128 devices in a mesh: dp: 8 (over z, y_lo), expert: 16 (over x, y_hi, core).
Axes of the slice: x: 4, y: 4 (y_hi: 2, y_lo: 2; y = y_hi * 2 + y_lo), z: 4, core: 2. Of those that a mesh axis runs over, the one named last changes fastest.
Arguments:
- tokens: bfloat16 [32768, 2048], P(('dp', 'expert')), may hold values from -6 to 6
- out_grad: bfloat16 [32768, 2048], P(('dp', 'expert')), may hold values from -6 to 6
- expert_ids: int32 [32768, 2], P(('dp', 'expert')), may hold values from 0 to 15, all different within a row; in each aligned block of 256 rows (0 to 255, 256 to 511, ...) at most 48 rows name the same one
- gate_values: bfloat16 [32768, 2], P(('dp', 'expert')), may hold values from 0.049804688 to 0.59765625
- master_gate_up: float32 [16, 2048, 1536], P('expert', 'dp'), may hold values from -4 to 4
- master_down: float32 [16, 768, 2048], P('expert', 'dp'), may hold values from -4 to 4
- moment_gate_up: float32 [16, 2048, 1536], P('expert', 'dp'), may hold values from -4 to 4
- moment_down: float32 [16, 768, 2048], P('expert', 'dp'), may hold values from -4 to 4
- second_gate_up: float32 [16, 2048, 1536], P('expert', 'dp'), may hold values from 0.003 to 0.006
- second_down: float32 [16, 768, 2048], P('expert', 'dp'), may hold values from 0.003 to 0.006
Outputs:
- input_grad: bfloat16 [32768, 2048], P(('dp', 'expert'))
- gate_grad: bfloat16 [32768, 2], P(('dp', 'expert'))
- new_gate_up: bfloat16 [16, 2048, 1536], P('expert')
- new_down: bfloat16 [16, 768, 2048], P('expert')
- master_gate_up_next: float32 [16, 2048, 1536], P('expert', 'dp')
- master_down_next: float32 [16, 768, 2048], P('expert', 'dp')
- moment_gate_up_next: float32 [16, 2048, 1536], P('expert', 'dp')
- moment_down_next: float32 [16, 768, 2048], P('expert', 'dp')
- second_gate_up_next: float32 [16, 2048, 1536], P('expert', 'dp')
- second_down_next: float32 [16, 768, 2048], P('expert', 'dp')
The draws below stay inside these ranges and needn't reach their ends.
Inputs may be any that keep to these rules, and one draw needn't show every extreme that they name: `expert_ids`: each token names 2 different experts. Among the rows of one device at most 48 routes name one expert, and in every draw some expert receives exactly 48 routes from some device.
All inputs are finite; a program needn't handle non-finite values.
Results may differ from the reference program's by a relative error of at most 0.028.
Values may be sent and summed in bfloat16 or wider, within the bound.
No kernel may reach another device: no remote copies, remote signals or barrier semaphores. Data moves between devices by JAX's collectives and lax.ppermute only.
A program may use at most 128 MiB of HBM per device.

```python
import math
import jax
import jax.numpy as jnp
import numpy as np
from jax import lax

D = 2048
FF = 768
TOK_DEV = 256
TOP = 2
EXPERTS = 16
TOKENS = 32768
CAP = 48
N_DP = 8
N_EXPERT = 16


def signed_moment(key, shape, power):
    sign_key, size_key = jax.random.split(key)
    positive = jax.random.bernoulli(sign_key, 0.5, shape)
    sign_value = jnp.where(positive, 1.0, -1.0).astype(jnp.float32)
    base = jax.random.uniform(size_key, shape, jnp.float32, 0.0, 1.0)
    magnitude = 2.5 + 1.5 * base ** power
    return sign_value * magnitude


def draw_moment_gate_up(key, part):
    key = jax.random.fold_in(key, 11)
    return signed_moment(key, (EXPERTS, D, 2 * FF), 1.0)


def draw_moment_down(key, part):
    key = jax.random.fold_in(key, 23)
    return signed_moment(key, (EXPERTS, FF, D), 1.0)


def block_scale(key, dims, shards, low, top_value):
    level = 1.0
    for axis_at, shards_of in shards:
        draws = jax.random.uniform(jax.random.fold_in(jax.random.fold_in(key, 6), axis_at), (shards_of,), jnp.float32, low / len(shards), top_value / len(shards))
        level = level * jnp.repeat(jnp.exp(draws), dims[axis_at] // shards_of).reshape((-1,) + (1,) * (len(dims) - 1 - axis_at))
    return level


def deal_out(own_key, own, number, rows, number_of, top, bound, skew):
    order = jax.random.permutation(own_key, number_of)
    crowded, common = shares(number_of, rows * top, bound, skew, True), shares(number_of, rows * top, bound, skew, False)
    places = jnp.arange(number_of)

    def named(tallies, turn):
        used = int((tallies > 0).sum())
        fixed = max(1, used // 4)
        passed = fixed + (places - fixed + turn * (used - fixed)) % max(1, number_of - fixed)
        return jnp.zeros((number_of,), jnp.int32).at[order[jnp.where(places < fixed, places, passed)]].set(jnp.asarray(tallies, jnp.int32))

    tallies = jnp.where(number % 4 == 0, named(crowded, number // 4), named(common, number - number // 4 - 1))
    mixed = jax.random.permutation(jax.random.fold_in(own, 3), number_of)
    source_of, receiver = mixed[0:number_of // 2 * 2:2], mixed[1:number_of // 2 * 2:2]
    slack = jnp.minimum(tallies[source_of] - 1, bound - tallies[receiver]) // 2
    slack = jnp.where((source_of == order[0]) | (receiver == order[0]) | (tallies[receiver] == 0), 0, jnp.maximum(slack, 0))
    passed = jax.random.randint(jax.random.fold_in(own, 4), (number_of // 2,), 0, 1 << 20) % (slack + 1)
    tallies = tallies.at[source_of].add(-passed).at[receiver].add(passed)
    members = jnp.searchsorted(jnp.cumsum(tallies), jnp.arange(rows * top), side="right").astype(jnp.int32)
    table = members.reshape(top, rows).T
    table = table[jax.random.permutation(jax.random.fold_in(own, 1), rows)]
    turn = jax.random.randint(jax.random.fold_in(own, 2), (rows, 1), 0, top)
    return jnp.take_along_axis(table, (jnp.arange(top)[None, :] + turn) % top, axis=1)


def shares(amount, total, most, slope, full):
    loads = [(1 << 20) // math.isqrt(standing ** slope) + 1 for standing in range(1, amount + 1)]
    largest = most if full else min(most, max(-(-total // amount), total * loads[0] // sum(loads)))
    least = 1 if total - largest >= amount - 1 else 0
    counts, surplus = [largest] + [least] * (amount - 1), total - largest - least * (amount - 1)
    while surplus > 0:
        movable = [i for i in range(1, amount) if counts[i] < largest] or [i for i in range(1, amount) if counts[i] < most]
        mass, left = sum([loads[i] for i in movable]), surplus
        for i in movable:
            addition = min(most - counts[i], max(1, left * loads[i] // mass), surplus)
            counts[i] = counts[i] + addition
            surplus = surplus - addition
    return np.array(counts)


def gaussian(stream_key, dims, scale, most, cuts=(), held_as=jnp.bfloat16):
    entries = jax.random.normal(stream_key, dims, jnp.float32) * scale
    if len(cuts) > 0:
        entries = block_scale(stream_key, dims, cuts, -0.22, 0.18) * entries
    return jnp.clip(entries, min=-most, max=most).astype(held_as)


def setup_inputs(seed: int = 0) -> dict:
    streams_of = jax.random.split(jax.random.key(seed), 11)
    tokens = gaussian(streams_of[0], (TOKENS, D), 1.0, 6.0, ((0, 128),))
    out_grad = gaussian(streams_of[1], (TOKENS, D), 1.0, 6.0, ((0, 128),))
    expert_ids_keys = jax.random.split(jax.random.fold_in(streams_of[2], 1), TOKENS // TOK_DEV)
    expert_ids_turns = jax.random.permutation(jax.random.fold_in(streams_of[2], 3), TOKENS // TOK_DEV)
    expert_ids = jax.vmap(lambda own, number: deal_out(jax.random.fold_in(streams_of[2], 2), own, number, TOK_DEV, EXPERTS, TOP, CAP, 2))(expert_ids_keys, expert_ids_turns).reshape((TOKENS, TOP))
    gate_values = jnp.clip(jnp.exp(math.log(0.59765625) - 2.4849066 * jax.random.uniform(streams_of[3], (TOKENS, TOP), jnp.float32) ** block_scale(streams_of[3], (TOKENS, TOP), ((0, 128),), -0.2, 0.2)), 0.049804688, 0.59765625).astype(jnp.bfloat16)
    master_gate_up = gaussian(streams_of[4], (EXPERTS, D, 2 * FF), 1.0, 4.0, ((0, 16), (1, 8)), jnp.float32)
    master_down = gaussian(streams_of[5], (EXPERTS, FF, D), 1.0, 4.0, ((0, 16), (1, 8)), jnp.float32)
    moment_gate_up = draw_moment_gate_up(jax.random.fold_in(streams_of[10], 71), 0)
    moment_down = draw_moment_down(jax.random.fold_in(streams_of[10], 71), 0)
    second_gate_up = jnp.clip(jnp.exp(math.log(0.006) - 0.6931472 * jax.random.uniform(streams_of[8], (EXPERTS, D, 2 * FF), jnp.float32) ** block_scale(streams_of[8], (EXPERTS, D, 2 * FF), ((0, 16), (1, 8)), -0.2, 0.2)), 0.003, 0.006)
    second_down = jnp.clip(jnp.exp(math.log(0.006) - 0.6931472 * jax.random.uniform(streams_of[9], (EXPERTS, FF, D), jnp.float32) ** block_scale(streams_of[9], (EXPERTS, FF, D), ((0, 16), (1, 8)), -0.2, 0.2)), 0.003, 0.006)
    return dict(tokens=tokens, out_grad=out_grad, expert_ids=expert_ids, gate_values=gate_values, master_gate_up=master_gate_up, master_down=master_down, moment_gate_up=moment_gate_up, moment_down=moment_down, second_gate_up=second_gate_up, second_down=second_down)


beta_first = 0.9
beta_second = 0.95
learn_rate = 0.01
weight_decay = 0.1
adam_epsilon = 1e-08
bias_first = 0.9999734386
bias_second = 0.9940794708

def expert_rows(in_rows, grad_rows, gate_rows, w_gate_up, w_down):
    hidden = w_down.shape[0]
    scale_in = in_rows.shape[1] ** (-0.5)
    scale_out = hidden ** (-0.5)
    projected = scale_in * jnp.dot(in_rows, w_gate_up, preferred_element_type=jnp.float32)
    gate_part = projected[:, :hidden]
    up_part = projected[:, hidden:]
    sig_gate = jax.nn.sigmoid(gate_part)
    swish_gate = gate_part * sig_gate
    hidden_act = (swish_gate * up_part).astype(jnp.bfloat16)
    expert_out = scale_out * jnp.dot(hidden_act, w_down, preferred_element_type=jnp.float32)
    gate_score = lax.optimization_barrier(jnp.sum(grad_rows.astype(jnp.float32) * expert_out, axis=1)).astype(jnp.bfloat16)
    scaled = (gate_rows.astype(jnp.float32)[:, None] * grad_rows.astype(jnp.float32)).astype(jnp.bfloat16)
    grad_act = scale_out * lax.dot_general(scaled, w_down, (((1,), (1,)), ((), ())), preferred_element_type=jnp.float32)
    grad_gate = grad_act * up_part * sig_gate * (1.0 + gate_part * (1.0 - sig_gate))
    grad_up = grad_act * swish_gate
    grad_proj = jnp.concatenate([grad_gate, grad_up], axis=1).astype(jnp.bfloat16)
    grad_route = (scale_in * lax.dot_general(grad_proj, w_gate_up, (((1,), (1,)), ((), ())), preferred_element_type=jnp.float32)).astype(jnp.bfloat16)
    return (hidden_act, scaled, grad_proj, grad_route, gate_score)

def adam_update(master, moment, second, grad):
    moment_next = beta_first * moment + (1.0 - beta_first) * grad
    second_next = beta_second * second + (1.0 - beta_second) * grad * grad
    step_size = moment_next / bias_first / (jnp.sqrt(second_next / bias_second) + adam_epsilon)
    master_next = master - learn_rate * (step_size + weight_decay * master)
    return (master_next, moment_next, second_next)

def reference(tokens, out_grad, expert_ids, gate_values, master_gate_up, master_down, moment_gate_up, moment_down, second_gate_up, second_down):
    per_rep = TOKENS // N_DP
    route_count = per_rep * TOP
    slot_rows = N_EXPERT * CAP
    weights_gate_up = master_gate_up.astype(jnp.bfloat16)
    weights_down = master_down.astype(jnp.bfloat16)
    scale_in = D ** (-0.5)
    scale_out = FF ** (-0.5)

    def replica(totals, rep_index):
        start = (rep_index * per_rep).astype(jnp.int32)
        in_rep = lax.dynamic_slice_in_dim(tokens, start, per_rep, 0)
        grad_rep = lax.dynamic_slice_in_dim(out_grad, start, per_rep, 0)
        ids_rep = lax.dynamic_slice_in_dim(expert_ids, start, per_rep, 0).reshape(route_count)
        gates_rep = lax.dynamic_slice_in_dim(gate_values, start, per_rep, 0).reshape(route_count)

        def one_expert(carry, expert_index):
            grad_acc, score_acc = carry
            sort_key = jnp.where(ids_rep == expert_index, 0, 1).astype(jnp.int32)
            order = jnp.argsort(sort_key, stable=True)[:slot_rows].astype(jnp.int32)
            valid = sort_key[order] == 0
            tok_index = (order // TOP).astype(jnp.int32)
            in_rows = jnp.where(valid[:, None], in_rep[tok_index], jnp.zeros((), jnp.bfloat16))
            grad_rows = jnp.where(valid[:, None], grad_rep[tok_index], jnp.zeros((), jnp.bfloat16))
            gate_rows = jnp.where(valid, gates_rep[order], jnp.zeros((), jnp.bfloat16))
            hidden_act, scaled, grad_proj, grad_route, gate_score = expert_rows(in_rows, grad_rows, gate_rows, weights_gate_up[expert_index], weights_down[expert_index])
            part_down = (scale_out * lax.dot_general(hidden_act, scaled, (((0,), (0,)), ((), ())), preferred_element_type=jnp.float32)).astype(jnp.bfloat16)
            part_gate_up = (scale_in * lax.dot_general(in_rows, grad_proj, (((0,), (0,)), ((), ())), preferred_element_type=jnp.float32)).astype(jnp.bfloat16)
            target = jnp.where(valid, order, route_count).astype(jnp.int32)
            grad_acc = grad_acc.at[target].set(grad_route, mode='drop')
            score_acc = score_acc.at[target].set(gate_score, mode='drop')
            return ((grad_acc, score_acc), (part_gate_up, part_down))
        start_carry = (jnp.zeros((route_count, D), jnp.bfloat16), jnp.zeros((route_count,), jnp.bfloat16))
        (grad_routes, score_routes), (parts_gate_up, parts_down) = lax.scan(one_expert, start_carry, jnp.arange(EXPERTS, dtype=jnp.int32))
        totals = (totals[0] + parts_gate_up.astype(jnp.float32), totals[1] + parts_down.astype(jnp.float32))
        return (totals, (grad_routes, score_routes))
    zero_totals = (jnp.zeros((EXPERTS, D, 2 * FF), jnp.float32), jnp.zeros((EXPERTS, FF, D), jnp.float32))
    (grad_gate_up, grad_down), (grad_routes, score_routes) = lax.scan(replica, zero_totals, jnp.arange(N_DP, dtype=jnp.int32))
    input_grad = lax.optimization_barrier(jnp.sum(grad_routes.reshape(TOKENS, TOP, D).astype(jnp.float32), axis=1)).astype(jnp.bfloat16)
    gate_grad = score_routes.reshape(TOKENS, TOP)
    master_gu_next, moment_gu_next, second_gu_next = adam_update(master_gate_up, moment_gate_up, second_gate_up, grad_gate_up)
    master_dn_next, moment_dn_next, second_dn_next = adam_update(master_down, moment_down, second_down, grad_down)
    return (input_grad, gate_grad, master_gu_next.astype(jnp.bfloat16), master_dn_next.astype(jnp.bfloat16), master_gu_next, master_dn_next, moment_gu_next, moment_dn_next, second_gu_next, second_dn_next)
```

```python
import jax
import jax.numpy as jnp
from jax import lax
from jax.sharding import PartitionSpec as P

beta_first = 0.9
beta_second = 0.95
learn_rate = 0.01
weight_decay = 0.1
adam_epsilon = 1e-08
bias_first = 0.9999734386
bias_second = 0.9940794708

F32 = jnp.float32
BF16 = jnp.bfloat16

Z_UP = [(i, (i + 2) % 8) for i in range(8)]
Z_DOWN = [(i, (i - 2) % 8) for i in range(8)]
Y_SWAP = [(i, i ^ 1) for i in range(8)]
X_UP = [(i, (i + 4) % 16) for i in range(16)]
X_DOWN = [(i, (i - 4) % 16) for i in range(16)]
X_FAR = [(i, (i + 8) % 16) for i in range(16)]
YH_SWAP = [(i, i ^ 2) for i in range(16)]
CORE_SWAP = [(i, i ^ 1) for i in range(16)]


def z_up(a):
    return lax.ppermute(a, "dp", Z_UP)


def z_down(a):
    return lax.ppermute(a, "dp", Z_DOWN)


def y_swap(a):
    return lax.ppermute(a, "dp", Y_SWAP)


def x_up(a):
    return lax.ppermute(a, "expert", X_UP)


def x_down(a):
    return lax.ppermute(a, "expert", X_DOWN)


def x_far(a):
    return lax.ppermute(a, "expert", X_FAR)


def yh_swap(a):
    return lax.ppermute(a, "expert", YH_SWAP)


def core_swap(a):
    return lax.ppermute(a, "expert", CORE_SWAP)


def place(full, block, shard):
    return lax.dynamic_update_slice(full, block, (shard * block.shape[0], 0))


def gather_shards(own, z, y):
    rows = own.shape[0]
    half = rows // 2
    full = jnp.zeros((8 * rows, own.shape[1]), own.dtype)
    for dy, block in ((0, own), (1, y_swap(own))):
        below = z_up(block)
        above = z_down(block)
        far_first = z_up(below[:half])
        far_last = z_down(above[half:])
        column = y ^ dy
        full = place(full, block, z * 2 + column)
        full = place(full, below, ((z + 3) % 4) * 2 + column)
        full = place(full, above, ((z + 1) % 4) * 2 + column)
        far = (((z + 2) % 4) * 2 + column) * 2
        full = place(full, far_first, far)
        full = place(full, far_last, far + 1)
    return full


def scatter_sum(block_of):
    sums = []
    for dy in (1, 0):
        far = block_of(2, dy)
        half = far.shape[0] // 2
        up_first = z_up(far[:half])
        down_last = z_down(far[half:])
        up_block = block_of(1, dy)
        down_block = block_of(-1, dy)
        up_sum = (up_block[:half].astype(F32) + up_first.astype(F32)).astype(BF16)
        down_sum = (down_block[half:].astype(F32) + down_last.astype(F32)).astype(BF16)
        from_below = z_up(jnp.concatenate([up_sum, up_block[half:]], axis=0))
        from_above = z_down(jnp.concatenate([down_block[:half], down_sum], axis=0))
        sums.append(
            block_of(0, dy).astype(F32) + from_below.astype(F32) + from_above.astype(F32)
        )
    other, own = sums
    return own + y_swap(other.astype(BF16)).astype(F32)


def adam_update(master, moment, second, grad):
    moment_next = beta_first * moment + (1.0 - beta_first) * grad
    second_next = beta_second * second + (1.0 - beta_second) * grad * grad
    step_size = moment_next / bias_first / (jnp.sqrt(second_next / bias_second) + adam_epsilon)
    master_next = master - learn_rate * (step_size + weight_decay * master)
    return (master_next, moment_next, second_next)


def local(
    tokens,
    out_grad,
    expert_ids,
    gate_values,
    master_gate_up,
    master_down,
    moment_gate_up,
    moment_down,
    second_gate_up,
    second_down,
):
    experts = 16
    tok_count, width = tokens.shape
    hidden = 768
    cap = 48
    route_count = 2 * tok_count
    scale_in = width ** (-0.5)
    scale_out = hidden ** (-0.5)
    r = lax.axis_index("dp")
    e = lax.axis_index("expert")
    z, y = r // 2, r % 2
    x, hc = e // 4, e % 4

    w_gate_up = gather_shards(master_gate_up[0].astype(BF16), z, y)
    w_down = gather_shards(master_down[0].astype(BF16), z, y)

    route_ids = expert_ids.reshape(route_count)
    onehot = (route_ids[:, None] == jnp.arange(experts, dtype=jnp.int32)[None, :]).astype(jnp.int32)
    before = jnp.cumsum(onehot, axis=0) - onehot
    position = route_ids * cap + jnp.sum(before * onehot, axis=1)
    pos_own = position.reshape(tok_count, 2).T
    pos_core = core_swap(pos_own)
    pos_yh = yh_swap(pos_own)
    pos_yhc = core_swap(pos_yh)

    slots = jnp.arange(experts * cap, dtype=jnp.int32)
    send_gate = jnp.sum(
        jnp.where(
            slots[:, None] == position[None, :],
            gate_values.reshape(1, route_count).astype(F32),
            0.0,
        ),
        axis=1,
    ).astype(BF16)
    gate_block = lax.all_to_all(
        send_gate.reshape(experts, cap), "expert", split_axis=0, concat_axis=0, tiled=True
    )

    dx = jnp.array([0, 1, 3, 2], jnp.int32)
    target = ((((x + dx) % 4) * 4 + hc) * cap)[:, None] + jnp.arange(cap, dtype=jnp.int32)[None, :]

    def pick(pos_pair):
        pos = jnp.stack(pos_pair)
        hit = (pos[:, 0][None, None] == target[:, :, None, None]) | (
            pos[:, 1][None, None] == target[:, :, None, None]
        )
        same = jnp.arange(2)[:, None] == jnp.arange(2)[None, :]
        full = hit[:, None] & same[None, :, None, :, None]
        return full.astype(BF16).reshape(8 * cap, 2 * tok_count)

    pick_near = pick((pos_own, pos_core))
    pick_far = pick((pos_yh, pos_yhc))

    def spread(rows):
        near = jnp.concatenate([rows, core_swap(rows)], axis=0)
        other = yh_swap(rows)
        far = jnp.concatenate([other, core_swap(other)], axis=0)
        got = []
        for chosen, block in ((pick_near, near), (pick_far, far)):
            sent = jnp.dot(chosen, block, preferred_element_type=F32).astype(BF16)
            sent = sent.reshape(4, 2 * cap, width)
            got.append((sent[0], x_up(sent[1]), x_down(sent[2]), x_far(sent[3])))
        return jnp.concatenate([got[s][j] for j in range(4) for s in range(2)], axis=0)

    in_rows = spread(tokens)
    grad_rows = spread(out_grad)
    offsets = jnp.array([0, 3, 1, 2], jnp.int32)
    source = (
        (((x + offsets) % 4) * 4)[:, None] + (hc ^ jnp.arange(4, dtype=jnp.int32))[None, :]
    ).reshape(16)
    gate_rows = gate_block[source].reshape(experts * cap)

    projected = scale_in * jnp.dot(in_rows, w_gate_up, preferred_element_type=F32)
    gate_part = projected[:, :hidden]
    up_part = projected[:, hidden:]
    sig_gate = jax.nn.sigmoid(gate_part)
    swish_gate = gate_part * sig_gate
    hidden_act = (swish_gate * up_part).astype(BF16)
    scaled = (gate_rows.astype(F32)[:, None] * grad_rows.astype(F32)).astype(BF16)

    contract_rows = (((0,), (0,)), ((), ()))
    part_down = (
        scale_out
        * lax.dot_general(hidden_act, scaled, contract_rows, preferred_element_type=F32)
    ).astype(BF16)

    def down_block(dz, dy):
        shard = ((z + dz) % 4) * 2 + (y ^ dy)
        return lax.dynamic_slice(part_down, (shard * 96, 0), (96, width))

    grad_down = scatter_sum(down_block)

    grad_act = scale_out * lax.dot_general(
        scaled, w_down, (((1,), (1,)), ((), ())), preferred_element_type=F32
    )
    grad_gate = grad_act * up_part * sig_gate * (1.0 + gate_part * (1.0 - sig_gate))
    grad_up = grad_act * swish_gate
    grad_proj = jnp.concatenate([grad_gate, grad_up], axis=1).astype(BF16)

    parts = {}
    for dz in (2, 1, -1, 0):
        plane = (z + dz) % 4
        columns = lax.dynamic_slice(in_rows, (0, plane * 512), (experts * cap, 512))
        parts[dz] = (
            scale_in
            * lax.dot_general(columns, grad_proj, contract_rows, preferred_element_type=F32)
        ).astype(BF16)

    def gate_up_block(dz, dy):
        return lax.dynamic_slice(parts[dz], ((y ^ dy) * 256, 0), (256, 2 * hidden))

    grad_gate_up = scatter_sum(gate_up_block)

    grad_route = (
        scale_in
        * lax.dot_general(
            grad_proj, w_gate_up, (((1,), (1,)), ((), ())), preferred_element_type=F32
        )
    ).astype(BF16)
    expert_out = scale_out * jnp.dot(hidden_act, w_down, preferred_element_type=F32)
    gate_score = jnp.sum(grad_rows.astype(F32) * expert_out, axis=1).astype(BF16)

    back = grad_route.reshape(4, 4 * cap, width)
    returned = jnp.concatenate(
        [back[0], x_down(back[1]), x_up(back[2]), x_far(back[3])], axis=0
    )
    pos_all = jnp.stack([pos_own, pos_core, pos_yh, pos_yhc])
    hit_back = (pos_all[:, 0, :, None, None] == target) | (pos_all[:, 1, :, None, None] == target)
    same_back = jnp.arange(4)[:, None] == jnp.arange(4)[None, :]
    choose = (hit_back[:, :, :, None, :] & same_back[:, None, None, :, None]).astype(BF16)
    partial = jnp.dot(
        choose.reshape(4 * tok_count, 16 * cap), returned, preferred_element_type=F32
    ).reshape(4, tok_count, width)
    swapped = core_swap(jnp.concatenate([partial[1], partial[3]], axis=0).astype(BF16)).astype(F32)
    own_sum = partial[0] + swapped[:tok_count]
    far_sum = partial[2] + swapped[tok_count:]
    input_grad = (own_sum + yh_swap(far_sum.astype(BF16)).astype(F32)).astype(BF16)

    home = jnp.zeros((16,), jnp.int32).at[source].set(jnp.arange(16, dtype=jnp.int32))
    score_back = lax.all_to_all(
        gate_score.reshape(experts, cap)[home], "expert", split_axis=0, concat_axis=0, tiled=True
    )
    gate_grad = score_back.reshape(experts * cap)[position].reshape(tok_count, 2)

    master_dn_next, moment_dn_next, second_dn_next = adam_update(
        master_down[0], moment_down[0], second_down[0], grad_down
    )
    new_down = gather_shards(master_dn_next.astype(BF16), z, y)
    master_gu_next, moment_gu_next, second_gu_next = adam_update(
        master_gate_up[0], moment_gate_up[0], second_gate_up[0], grad_gate_up
    )
    new_gate_up = gather_shards(master_gu_next.astype(BF16), z, y)
    return (
        input_grad,
        gate_grad,
        new_gate_up[None],
        new_down[None],
        master_gu_next[None],
        master_dn_next[None],
        moment_gu_next[None],
        moment_dn_next[None],
        second_gu_next[None],
        second_dn_next[None],
    )


def solution(mesh):
    rows = P(("dp", "expert"), None)
    state = P("expert", "dp", None)
    whole = P("expert", None, None)
    return jax.shard_map(
        local,
        mesh=mesh,
        in_specs=(rows,) * 4 + (state,) * 6,
        out_specs=(rows, rows, whole, whole) + (state,) * 6,
        check_vma=False,
    )
```

```python
import jax
import jax.numpy as jnp
from jax import lax
from jax.experimental import pallas as pl
from jax.experimental.pallas import tpu as pltpu
from jax.sharding import PartitionSpec as P

beta_first = 0.9
beta_second = 0.95
learn_rate = 0.01
weight_decay = 0.1
adam_epsilon = 1e-08
bias_first = 0.9999734386
bias_second = 0.9940794708

F32 = jnp.float32
BF16 = jnp.bfloat16

Z_UP = [(i, (i + 2) % 8) for i in range(8)]
Z_DOWN = [(i, (i - 2) % 8) for i in range(8)]
Y_SWAP = [(i, i ^ 1) for i in range(8)]


def z_up(a):
    return lax.ppermute(a, "dp", Z_UP)


def z_down(a):
    return lax.ppermute(a, "dp", Z_DOWN)


def y_swap(a):
    return lax.ppermute(a, "dp", Y_SWAP)


def adam_update(master, moment, second, grad):
    moment_next = beta_first * moment + (1.0 - beta_first) * grad
    second_next = beta_second * second + (1.0 - beta_second) * grad * grad
    step_size = moment_next / bias_first / (jnp.sqrt(second_next / bias_second) + adam_epsilon)
    master_next = master - learn_rate * (step_size + weight_decay * master)
    return (master_next, moment_next, second_next)


CAP = 48
HALF_SLOTS = 8 * CAP
SLOTS = 16 * CAP
TOK = 256
WIDTH = 2048
EXTRA = 128
VMEM_LIMIT = 48 * 1024 * 1024
YH_SWAP = [(i, i ^ 2) for i in range(16)]
X_GROUPS = [[x * 4 + h * 2 + c for x in range(4) for c in range(2)] for h in range(2)]


def yh_swap(a):
    return lax.ppermute(a, "expert", YH_SWAP)


def exchange(rows):
    return lax.all_to_all(
        rows.reshape(8, rows.shape[0] // 8, rows.shape[1]),
        "expert",
        split_axis=0,
        concat_axis=0,
        axis_index_groups=X_GROUPS,
        tiled=True,
    ).reshape(rows.shape)


def one_hots(aux_ref):
    number = lax.broadcasted_iota(jnp.int32, (HALF_SLOTS, TOK), 0)
    pos = aux_ref[0:2, :].astype(jnp.int32)
    return number == pos[0:1, :], number == pos[1:2, :]


def as_bf16(mask):
    return mask.astype(F32).astype(BF16)


def route_kernel(half_ref, ids_ref, gate_ref, near_ref, far_ref):
    ids0, ids1 = ids_ref[0:1, :], ids_ref[1:2, :]
    expert = lax.broadcasted_iota(jnp.int32, (16, TOK), 0)
    hit0 = expert == ids0
    hit1 = expert == ids1
    ahead = as_bf16(
        lax.broadcasted_iota(jnp.int32, (TOK, TOK), 0)
        < lax.broadcasted_iota(jnp.int32, (TOK, TOK), 1)
    )
    one0 = hit0.astype(F32)
    before0 = jnp.dot(as_bf16(hit0), ahead, preferred_element_type=F32)
    before1 = jnp.dot(as_bf16(hit1), ahead, preferred_element_type=F32)
    before1 = before1 + jnp.sum(one0, axis=1, keepdims=True)
    slot0 = jnp.sum(jnp.where(hit0, before0, 0.0), axis=0, keepdims=True)
    slot1 = jnp.sum(jnp.where(hit1, before1, 0.0), axis=0, keepdims=True)

    def place_in(ids, slot):
        return (((ids >> 2) * 2 + (ids & 1)) * CAP).astype(F32) + slot

    place0, place1 = place_in(ids0, slot0), place_in(ids1, slot1)
    here0 = ((ids0 >> 1) & 1) == half_ref[0]
    here1 = ((ids1 >> 1) & 1) == half_ref[0]
    near_ref[0:1, :] = jnp.where(here0, place0, -1.0)
    near_ref[1:2, :] = jnp.where(here1, place1, -1.0)
    far_ref[0:1, :] = jnp.where(here0, -1.0, place0)
    far_ref[1:2, :] = jnp.where(here1, -1.0, place1)
    near_ref[2:4, :] = gate_ref[...]
    far_ref[2:4, :] = gate_ref[...]

    def back_in(ids, slot):
        return (((ids >> 2) * 2 + (ids & 1)) * 2 * CAP).astype(F32) + slot

    back0, back1 = back_in(ids0, slot0), back_in(ids1, slot1)
    near_ref[4:5, :] = jnp.where(here0, back0, -1.0)
    near_ref[5:6, :] = jnp.where(here1, back1, -1.0)
    far_ref[4:5, :] = jnp.where(here0, -1.0, back0 + CAP)
    far_ref[5:6, :] = jnp.where(here1, -1.0, back1 + CAP)
    near_ref[6:8, :] = gate_ref[...]
    far_ref[6:8, :] = gate_ref[...]


def fill_tokens(column_ref, chosen, tok_ref, out_ref):
    for i in range(8):
        source = pl.multiple_of(column_ref[i] * 256, 256)
        out_ref[:, i * 256 : (i + 1) * 256] = jnp.dot(
            chosen, tok_ref[:, pl.ds(source, 256)], preferred_element_type=F32
        ).astype(BF16)


def fill_grads(first, second, chosen, aux_ref, grad_ref, out_ref, at):
    for i in range(8):
        out_ref[:, at + i * 256 : at + (i + 1) * 256] = jnp.dot(
            chosen, grad_ref[:, i * 256 : (i + 1) * 256], preferred_element_type=F32
        ).astype(BF16)
    gate = jnp.sum(
        jnp.where(first, aux_ref[2:3, :], 0.0) + jnp.where(second, aux_ref[3:4, :], 0.0),
        axis=1,
        keepdims=True,
    )
    out_ref[:, at + WIDTH :] = jnp.broadcast_to(gate, (HALF_SLOTS, EXTRA)).astype(BF16)


def spread_kernel(column_ref, aux_ref, tok_ref, grad_ref, out_ref):
    first, second = one_hots(aux_ref)
    chosen = as_bf16(first | second)
    fill_tokens(column_ref, chosen, tok_ref, out_ref)
    fill_grads(first, second, chosen, aux_ref, grad_ref, out_ref, WIDTH)


def spread_tokens_kernel(column_ref, aux_ref, tok_ref, out_ref):
    first, second = one_hots(aux_ref)
    fill_tokens(column_ref, as_bf16(first | second), tok_ref, out_ref)


def spread_grads_kernel(aux_ref, grad_ref, out_ref):
    first, second = one_hots(aux_ref)
    fill_grads(first, second, as_bf16(first | second), aux_ref, grad_ref, out_ref, 0)


def collect_kernel(near_aux_ref, far_aux_ref, rows_ref, near_ref, far_ref):
    to_tokens = (((0,), (0,)), ((), ()))
    number = lax.broadcasted_iota(jnp.int32, (SLOTS, TOK), 0)
    for aux_ref, out_ref in ((near_aux_ref, near_ref), (far_aux_ref, far_ref)):
        pos = aux_ref[4:6, :].astype(jnp.int32)
        first, second = number == pos[0:1, :], number == pos[1:2, :]
        out_ref[:, :WIDTH] = lax.dot_general(
            as_bf16(first | second),
            rows_ref[:, :WIDTH],
            to_tokens,
            preferred_element_type=F32,
        ).astype(out_ref.dtype)
        score = rows_ref[:, WIDTH:]
        score0 = lax.dot_general(as_bf16(first), score, to_tokens, preferred_element_type=F32)
        score1 = lax.dot_general(as_bf16(second), score, to_tokens, preferred_element_type=F32)
        lane = lax.broadcasted_iota(jnp.int32, (TOK, EXTRA), 1)
        out_ref[:, WIDTH:] = jnp.where(lane == 0, score0, score1).astype(out_ref.dtype)


def finish_kernel(column_ref, near_ref, far_ref, out_ref, score_ref):
    for i in range(8):
        target = pl.multiple_of(column_ref[i] * 256, 256)
        part = slice(i * 256, (i + 1) * 256)
        out_ref[:, pl.ds(target, 256)] = (near_ref[:, part] + far_ref[:, part].astype(F32)).astype(
            BF16
        )
    score_ref[...] = (near_ref[:, WIDTH:] + far_ref[:, WIDTH:].astype(F32)).astype(BF16)


HIDDEN = 768
SCALE_IN = WIDTH ** (-0.5)
SCALE_OUT = HIDDEN ** (-0.5)
BOTH = (slice(0, HALF_SLOTS), slice(HALF_SLOTS, SLOTS))
TN = (((0,), (0,)), ((), ()))
NT = (((1,), (1,)), ((), ()))


def dot(a, b, dims=(((1,), (0,)), ((), ()))):
    return lax.dot_general(a, b, dims, preferred_element_type=F32)


def pack_down(down):
    tail = [down[32 * j : 32 * j + 32, 1536:] for j in range(3)]
    return jnp.concatenate([down[:, :1536], jnp.concatenate(tail, axis=1)], axis=0)


def unpack_down(packed):
    tail = [packed[96:128, 512 * j : 512 * j + 512] for j in range(3)]
    return jnp.concatenate([packed[:96], jnp.concatenate(tail, axis=0)], axis=1)


def gate_up_parts(refs):
    own, other, below, above, up2, down2, up3, down3 = refs
    return [
        [(own, 0, 256)],
        [(other, 0, 256)],
        [(above, 0, 256)],
        [(down2, 192, 256)],
        [(up2, 0, 128), (down2, 0, 128)],
        [(up3, 0, 128), (down3, 0, 128)],
        [(below, 0, 256)],
        [(up2, 192, 256)],
    ]


def down_parts(refs):
    own, other, below, above, up2, down2, up3, down3 = refs
    return [
        [(own, 256, 128)],
        [(other, 256, 128)],
        [(above, 256, 128)],
        [(down2, 448, 128)],
        [(up2, 128, 64), (down2, 128, 64)],
        [(up3, 128, 64), (down3, 128, 64)],
        [(below, 256, 128)],
        [(up2, 448, 128)],
    ]


def read(pieces, columns):
    got = [ref[at : at + rows, columns] for ref, at, rows in pieces]
    return got[0] if len(got) == 1 else jnp.concatenate(got, axis=0)


def forward_kernel(column_ref, near_ref, far_ref, *refs):
    weights, (act_ref, slope_ref, swish_ref, down_ref) = refs[:8], refs[8:]
    blocks = gate_up_parts(weights)
    for rows, x_ref in zip(BOTH, (near_ref, far_ref)):
        for f in range(3):
            lo = slice(f * 256, f * 256 + 256)
            hi = slice(HIDDEN + f * 256, HIDDEN + f * 256 + 256)
            gate = jnp.zeros((HALF_SLOTS, 256), F32)
            up = jnp.zeros((HALF_SLOTS, 256), F32)
            for i, pieces in enumerate(blocks):
                x = x_ref[:, i * 256 : i * 256 + 256]
                gate += dot(x, read(pieces, lo))
                up += dot(x, read(pieces, hi))
            gate = gate * SCALE_IN
            up = up * SCALE_IN
            sig = jax.nn.sigmoid(gate)
            swish = gate * sig
            act_ref[rows, lo] = (swish * up).astype(BF16)
            slope_ref[rows, lo] = up * sig * (1.0 + gate * (1.0 - sig))
            swish_ref[rows, lo] = swish
    for i, pieces in enumerate(down_parts(weights)):
        row = pl.multiple_of(column_ref[i] * 96, 32)
        packed = read(pieces, slice(None))
        down_ref[pl.ds(row, 96), :1536] = packed[:96]
        for j in range(3):
            down_ref[pl.ds(row + 32 * j, 32), 1536:] = packed[96:128, 512 * j : 512 * j + 512]


def backward_kernel(
    column_ref,
    near_ref,
    far_in_ref,
    far_grad_ref,
    act_ref,
    slope_ref,
    swish_ref,
    down_ref,
    proj_ref,
    far_plane_ref,
    parts_ref,
    scaled_ref,
    whole_ref,
):
    for rows, grad_ref, at in ((BOTH[0], near_ref, WIDTH), (BOTH[1], far_grad_ref, 0)):
        gate = grad_ref[:, at + WIDTH : at + WIDTH + EXTRA].astype(F32)
        gate = gate[:, 0:1]
        for n in range(4):
            grad = grad_ref[:, at + n * 512 : at + n * 512 + 512].astype(F32)
            scaled_ref[rows, n * 512 : n * 512 + 512] = (gate * grad).astype(BF16)
    for rows in BOTH:
        for f in range(3):
            lo = slice(f * 256, f * 256 + 256)
            grad_act = SCALE_OUT * dot(scaled_ref[rows, :], down_ref[lo, :], NT)
            proj_ref[rows, lo] = (grad_act * slope_ref[rows, lo]).astype(BF16)
            proj_ref[rows, HIDDEN + f * 256 : HIDDEN + f * 256 + 256] = (
                grad_act * swish_ref[rows, lo]
            ).astype(BF16)
    plane_product(near_ref, far_in_ref, proj_ref, far_plane_ref, 2)
    for n in range(4):
        part = slice(n * 512, n * 512 + 512)
        for f in range(3):
            lo = slice(f * 256, f * 256 + 256)
            whole_ref[lo, part] = (SCALE_OUT * dot(act_ref[:, lo], scaled_ref[:, part], TN)).astype(
                BF16
            )
    for i in range(8):
        row = pl.multiple_of(column_ref[i] * 96, 32)
        parts_ref[i, 0:96, :] = whole_ref[pl.ds(row, 96), :1536]
        for j in range(3):
            parts_ref[i, 96:128, 512 * j : 512 * j + 512] = whole_ref[
                pl.ds(row + 32 * j, 32), 1536:
            ]


def plane_product(near_ref, far_ref, proj_ref, out_ref, k):
    for half in range(2):
        at = k * 512 + half * 256
        for n in range(3):
            part = slice(n * 512, n * 512 + 512)
            total = dot(near_ref[:, at : at + 256], proj_ref[BOTH[0], part], TN)
            total += dot(far_ref[:, at : at + 256], proj_ref[BOTH[1], part], TN)
            out_ref[half * 256 : half * 256 + 256, part] = (SCALE_IN * total).astype(BF16)


def planes_kernel(near_ref, far_ref, proj_ref, above_ref, below_ref, own_ref):
    for k, out_ref in ((1, above_ref), (3, below_ref), (0, own_ref)):
        plane_product(near_ref, far_ref, proj_ref, out_ref, k)


def back_kernel(near_ref, far_grad_ref, act_ref, proj_ref, down_ref, *refs):
    blocks, out_ref = gate_up_parts(refs[:8]), refs[8]
    for which, (rows, grad_ref, at) in enumerate(
        ((BOTH[0], near_ref, WIDTH), (BOTH[1], far_grad_ref, 0))
    ):

        def store(columns, value):
            value = value.astype(BF16)
            for i in range(8):
                out_ref[i * 96 + which * 48 : i * 96 + which * 48 + 48, columns] = value[
                    i * 48 : i * 48 + 48
                ]

        for i, pieces in enumerate(blocks):
            route = SCALE_IN * dot(proj_ref[rows, :], read(pieces, slice(None)), NT)
            store(slice(i * 256, i * 256 + 256), route)
        score = jnp.zeros((HALF_SLOTS, 1), F32)
        for n in range(8):
            part = slice(n * 256, n * 256 + 256)
            out = SCALE_OUT * dot(act_ref[rows, :], down_ref[:, part])
            grad = grad_ref[:, at + n * 256 : at + n * 256 + 256].astype(F32)
            score += jnp.sum(grad * out, axis=1, keepdims=True)
        store(slice(WIDTH, WIDTH + EXTRA), jnp.broadcast_to(score, (HALF_SLOTS, EXTRA)))


def add(*refs_or_values):
    total = refs_or_values[0].astype(F32)
    for value in refs_or_values[1:]:
        total = total + value.astype(F32)
    return total


def second_kernel(far_ref, above_ref, below_ref, parts_ref, up_ref, down_ref, y_ref, o_up, o_down):
    o_up[0:128] = add(above_ref[256:384], up_ref[...]).astype(BF16)
    o_up[128:256] = above_ref[384:512]
    o_up[256:384] = far_ref[0:128]
    o_up[384:448] = add(parts_ref[4, 0:64], y_ref[0:64]).astype(BF16)
    o_down[0:128] = below_ref[256:384]
    o_down[128:256] = add(below_ref[384:512], down_ref[...]).astype(BF16)
    o_down[256:384] = far_ref[128:256]
    o_down[384:448] = add(parts_ref[4, 64:128], y_ref[64:128]).astype(BF16)


def third_kernel(
    above_ref, below_ref, own_ref, parts_ref, up_ref, down_ref, y_ref, o_up, o_down, o_y
):
    o_up[0:128] = add(above_ref[0:128], up_ref[256:384]).astype(BF16)
    o_up[128:256] = above_ref[128:256]
    o_up[256:320] = add(parts_ref[2, 0:64], y_ref[0:64], up_ref[384:448]).astype(BF16)
    o_up[320:384] = add(parts_ref[2, 64:128], y_ref[64:128]).astype(BF16)
    o_down[0:128] = below_ref[0:128]
    o_down[128:256] = add(below_ref[128:256], down_ref[256:384]).astype(BF16)
    o_down[256:320] = add(parts_ref[6, 0:64], y_ref[128:192]).astype(BF16)
    o_down[320:384] = add(parts_ref[6, 64:128], y_ref[192:256], down_ref[384:448]).astype(BF16)
    o_y[0:256] = add(own_ref[256:512], up_ref[0:256], down_ref[0:256]).astype(BF16)
    o_y[256:384] = parts_ref[1]


def update_kernel(
    own_ref, parts_ref, up_ref, down_ref, y_ref, w_gu, w_dn, m_gu, m_dn, s_gu, s_dn, out_ref, sum_ref
):
    grad = add(own_ref[0:256], up_ref[0:256], down_ref[0:256], y_ref[0:256])
    out_ref[0:256] = adam_update(w_gu[...], m_gu[...], s_gu[...], grad)[0].astype(BF16)
    sum_ref[...] = add(parts_ref[0], up_ref[256:384], down_ref[256:384], y_ref[256:384])
    new = adam_update(
        w_dn[:, :1536], m_dn[:, :1536], s_dn[:, :1536], sum_ref[0:96, :]
    )[0]
    out_ref[256:352] = new.astype(BF16)
    for j in range(3):
        rows = slice(32 * j, 32 * j + 32)
        part = slice(512 * j, 512 * j + 512)
        new = adam_update(
            w_dn[rows, 1536:], m_dn[rows, 1536:], s_dn[rows, 1536:], sum_ref[96:128, part]
        )[0]
        out_ref[352:384, part] = new.astype(BF16)


def tie(*arrays):
    return lax.optimization_barrier(arrays)


def place(full, block, shard):
    return lax.dynamic_update_slice(full, block, (shard * block.shape[0], 0))


def assemble(blocks, z, y):
    rows, columns = blocks[(0, 0)].shape
    full = jnp.zeros((8 * rows, columns), BF16)
    for (k, dy), block in blocks.items():
        full = place(full, block, ((z + k) % 4) * 2 + (y ^ dy))
    return full


def bf(*shape):
    return jax.ShapeDtypeStruct(shape, BF16)


def f32(*shape):
    return jax.ShapeDtypeStruct(shape, F32)


def call(kernel, outs, inputs, scalars=0, scratch=(), flops=0):
    vmem = pl.BlockSpec(memory_space=pltpu.VMEM)
    smem = pl.BlockSpec(memory_space=pltpu.SMEM)
    moved = sum(a.size * a.dtype.itemsize for a in inputs) + sum(
        o.size * o.dtype.itemsize for o in outs
    )
    got = pl.pallas_call(
        kernel,
        out_shape=outs,
        in_specs=[smem] * scalars + [vmem] * (len(inputs) - scalars),
        out_specs=(vmem,) * len(outs),
        scratch_shapes=scratch,
        cost_estimate=pl.CostEstimate(flops=flops, bytes_accessed=moved, transcendentals=0),
        compiler_params=pltpu.CompilerParams(vmem_limit_bytes=VMEM_LIMIT),
    )(*inputs)
    return got if len(outs) > 1 else got[0]


def local(
    tokens,
    out_grad,
    expert_ids,
    gate_values,
    master_gate_up,
    master_down,
    moment_gate_up,
    moment_down,
    second_gate_up,
    second_down,
):
    r = lax.axis_index("dp")
    z, y = r // 2, r % 2
    order = [(k, dy) for k in range(4) for dy in range(2)]
    columns = jnp.stack([((z + k) % 4) * 2 + (y ^ dy) for k, dy in order])
    half = ((lax.axis_index("expert") >> 1) & 1).reshape(1)

    own = jnp.concatenate(
        [master_gate_up[0].astype(BF16), pack_down(master_down[0].astype(BF16))], axis=0
    )
    near_aux, far_aux = call(
        route_kernel,
        (f32(8, TOK), f32(8, TOK)),
        (half, expert_ids.T, gate_values.astype(F32).T),
        scalars=1,
    )
    near = exchange(
        call(
            spread_kernel,
            (bf(HALF_SLOTS, 2 * WIDTH + EXTRA),),
            (columns, near_aux, tokens, out_grad),
            scalars=1,
        )
    )
    below, above, other = z_up(own), z_down(own), y_swap(own)
    their_aux = yh_swap(far_aux)
    below, above, other, their_aux, tok_next = tie(below, above, other, their_aux, tokens)

    up2 = z_up(jnp.concatenate([below[:128], below[256:320], other], axis=0))
    down2 = z_down(jnp.concatenate([above[128:256], above[320:384], other], axis=0))
    their_tok = yh_swap(tok_next)
    their_tok, grad_next = tie(their_tok, out_grad)
    their_grad = yh_swap(grad_next)
    send_far = call(
        spread_tokens_kernel,
        (bf(HALF_SLOTS, WIDTH),),
        (columns, their_aux, their_tok),
        scalars=1,
    )
    send_far, near = tie(send_far, near)
    far_in = exchange(send_far)
    up2, down2, their_grad = tie(up2, down2, their_grad)

    up3 = z_up(jnp.concatenate([up2[192:320], up2[448:512]], axis=0))
    down3 = z_down(jnp.concatenate([down2[320:448], down2[512:576]], axis=0))
    send_far = call(spread_grads_kernel, (bf(HALF_SLOTS, WIDTH + EXTRA),), (their_aux, their_grad))
    send_far, far_in = tie(send_far, far_in)
    far_grad = exchange(send_far)
    up3, down3, far_in = tie(up3, down3, far_in)
    weights = (own, other, below, above, up2, down2, up3, down3)

    act, slope, swish, down = call(
        forward_kernel,
        (
            bf(SLOTS, HIDDEN),
            f32(SLOTS, HIDDEN),
            f32(SLOTS, HIDDEN),
            bf(HIDDEN, WIDTH),
        ),
        (columns, near, far_in) + weights,
        scalars=1,
        flops=4_800_000_000,
    )
    proj, far_plane, parts = call(
        backward_kernel,
        (bf(SLOTS, 2 * HIDDEN), bf(512, 1536), bf(8, 128, 1536)),
        (columns, near, far_in, far_grad, act, slope, swish, down),
        scalars=1,
        scratch=(pltpu.VMEM((SLOTS, WIDTH), BF16), pltpu.VMEM((HIDDEN, WIDTH), BF16)),
        flops=6_000_000_000,
    )

    t_up = z_up(far_plane[256:384])
    t_down = z_down(far_plane[384:512])
    t_y = y_swap(parts[5])
    above_plane, below_plane, own_plane = call(
        planes_kernel,
        (bf(512, 1536),) * 3,
        (near, far_in, proj),
        flops=3_600_000_000,
    )
    t_up, t_down, t_y, above_plane, below_plane, own_plane, late_proj = tie(
        t_up, t_down, t_y, above_plane, below_plane, own_plane, proj
    )
    s_up, s_down = call(
        second_kernel,
        (bf(448, 1536), bf(448, 1536)),
        (far_plane, above_plane, below_plane, parts, t_up, t_down, t_y),
    )
    s_y = jnp.concatenate([parts[3], parts[7]], axis=0)
    t_up, t_down, t_y = z_up(s_up), z_down(s_down), y_swap(s_y)
    back = call(
        back_kernel,
        (bf(SLOTS, WIDTH + EXTRA),),
        (near, far_grad, act, late_proj, down) + weights,
        flops=7_200_000_000,
    )
    t_up, t_down, t_y, back = tie(t_up, t_down, t_y, back)
    s_up, s_down, s_y = call(
        third_kernel,
        (bf(384, 1536),) * 3,
        (above_plane, below_plane, own_plane, parts, t_up, t_down, t_y),
    )
    t_up, t_down, t_y = z_up(s_up), z_down(s_down), y_swap(s_y)
    returned = exchange(back)
    t_up, t_down, t_y = tie(t_up, t_down, t_y)
    state = (
        master_gate_up[0],
        master_down[0],
        moment_gate_up[0],
        moment_down[0],
        second_gate_up[0],
        second_down[0],
    )
    new_own = call(
        update_kernel,
        (bf(384, 1536),),
        (own_plane, parts, t_up, t_down, t_y) + state,
        scratch=(pltpu.VMEM((128, 1536), F32),),
    )

    below, above, other = z_up(new_own), z_down(new_own), y_swap(new_own)
    grad_gate_up = add(own_plane[:256], t_up[:256], t_down[:256], t_y[:256])
    grad_down = unpack_down(add(parts[0], t_up[256:], t_down[256:], t_y[256:]))
    master_gu_next, moment_gu_next, second_gu_next = adam_update(
        state[0], state[2], state[4], grad_gate_up
    )
    master_dn_next, moment_dn_next, second_dn_next = adam_update(
        state[1], state[3], state[5], grad_down
    )
    below, above, other, returned = tie(below, above, other, returned)
    gu = {(0, 0): new_own[:256], (3, 0): below[:256], (1, 0): above[:256], (0, 1): other[:256]}
    dn = {(0, 0): new_own[256:], (3, 0): below[256:], (1, 0): above[256:], (0, 1): other[256:]}
    up2 = z_up(jnp.concatenate([below[:128], below[256:320], other[:256]], axis=0))
    down2 = z_down(jnp.concatenate([above[128:256], above[320:384], other[:256]], axis=0))
    side2 = y_swap(jnp.concatenate([above[256:], below[256:]], axis=0))
    near_sum, far_sum = call(
        collect_kernel,
        (f32(TOK, WIDTH + EXTRA), bf(TOK, WIDTH + EXTRA)),
        (near_aux, their_aux, returned),
        flops=1_700_000_000,
    )
    far_sum = yh_swap(far_sum)
    up2, down2, side2 = tie(up2, down2, side2)
    gu[(2, 0)] = jnp.concatenate([up2[:128], down2[:128]], axis=0)
    dn[(2, 0)] = jnp.concatenate([up2[128:192], down2[128:192]], axis=0)
    gu[(3, 1)], gu[(1, 1)] = up2[192:], down2[192:]
    dn[(1, 1)], dn[(3, 1)] = side2[:128], side2[128:]
    up3, down3, side3 = z_up(up2[192:320]), z_down(down2[320:448]), y_swap(dn[(2, 0)])
    gu[(2, 1)] = jnp.concatenate([up3, down3], axis=0)
    dn[(2, 1)] = side3
    new_gate_up = assemble(gu, z, y)
    new_down = assemble({at: unpack_down(block) for at, block in dn.items()}, z, y)

    input_grad, scores = call(
        finish_kernel,
        (bf(TOK, WIDTH), bf(TOK, EXTRA)),
        (columns, near_sum, far_sum),
        scalars=1,
    )
    gate_grad = scores[:, :2]
    return (
        input_grad,
        gate_grad,
        new_gate_up[None],
        new_down[None],
        master_gu_next[None],
        master_dn_next[None],
        moment_gu_next[None],
        moment_dn_next[None],
        second_gu_next[None],
        second_dn_next[None],
    )


def solution(mesh):
    rows = P(("dp", "expert"), None)
    state = P("expert", "dp", None)
    whole = P("expert", None, None)
    return jax.shard_map(
        local,
        mesh=mesh,
        in_specs=(rows,) * 4 + (state,) * 6,
        out_specs=(rows, rows, whole, whole) + (state,) * 6,
        check_vma=False,
    )
```

```python
import functools
import math

import jax
import jax.numpy as jnp
from jax import lax
from jax.experimental import pallas as pl
from jax.experimental.pallas import tpu as pltpu
from jax.sharding import PartitionSpec as P

beta_first = 0.9
beta_second = 0.95
learn_rate = 0.01
weight_decay = 0.1
adam_epsilon = 1e-08
bias_first = 0.9999734386
bias_second = 0.9940794708

F32 = jnp.float32
BF16 = jnp.bfloat16

Z_UP = [(i, (i + 2) % 8) for i in range(8)]
Z_DOWN = [(i, (i - 2) % 8) for i in range(8)]
Y_SWAP = [(i, i ^ 1) for i in range(8)]


def z_up(a):
    return lax.ppermute(a, "dp", Z_UP)


def z_down(a):
    return lax.ppermute(a, "dp", Z_DOWN)


def y_swap(a):
    return lax.ppermute(a, "dp", Y_SWAP)


def adam_update(master, moment, second, grad):
    moment_next = beta_first * moment + (1.0 - beta_first) * grad
    second_next = beta_second * second + (1.0 - beta_second) * grad * grad
    step_size = moment_next / bias_first / (jnp.sqrt(second_next / bias_second) + adam_epsilon)
    master_next = master - learn_rate * (step_size + weight_decay * master)
    return (master_next, moment_next, second_next)


CAP = 48
HALF_SLOTS = 8 * CAP
SLOTS = 16 * CAP
TOK = 256
WIDTH = 2048
EXTRA = 128
YH_SWAP = [(i, i ^ 2) for i in range(16)]
X_GROUPS = [[x * 4 + h * 2 + c for x in range(4) for c in range(2)] for h in range(2)]


def yh_swap(a):
    return lax.ppermute(a, "expert", YH_SWAP)


def exchange(rows):
    return lax.all_to_all(
        rows.reshape(8, rows.shape[0] // 8, rows.shape[1]),
        "expert",
        split_axis=0,
        concat_axis=0,
        axis_index_groups=X_GROUPS,
        tiled=True,
    ).reshape(rows.shape)


def one_hots(aux_ref):
    number = lax.broadcasted_iota(jnp.int32, (HALF_SLOTS, TOK), 0)
    pos = aux_ref[0:2, :].astype(jnp.int32)
    return number == pos[0:1, :], number == pos[1:2, :]


def as_bf16(mask):
    return mask.astype(F32).astype(BF16)


def route_kernel(half_ref, ids_ref, gate_ref, near_ref, far_ref):
    ids0, ids1 = ids_ref[0:1, :], ids_ref[1:2, :]
    expert = lax.broadcasted_iota(jnp.int32, (16, TOK), 0)
    hit0 = expert == ids0
    hit1 = expert == ids1
    ahead = as_bf16(
        lax.broadcasted_iota(jnp.int32, (TOK, TOK), 0)
        < lax.broadcasted_iota(jnp.int32, (TOK, TOK), 1)
    )
    one0 = hit0.astype(F32)
    before0 = jnp.dot(as_bf16(hit0), ahead, preferred_element_type=F32)
    before1 = jnp.dot(as_bf16(hit1), ahead, preferred_element_type=F32)
    before1 = before1 + jnp.sum(one0, axis=1, keepdims=True)
    slot0 = jnp.sum(jnp.where(hit0, before0, 0.0), axis=0, keepdims=True)
    slot1 = jnp.sum(jnp.where(hit1, before1, 0.0), axis=0, keepdims=True)

    def place_in(ids, slot):
        return (((ids >> 2) * 2 + (ids & 1)) * CAP).astype(F32) + slot

    place0, place1 = place_in(ids0, slot0), place_in(ids1, slot1)
    here0 = ((ids0 >> 1) & 1) == half_ref[0]
    here1 = ((ids1 >> 1) & 1) == half_ref[0]
    near_ref[0:1, :] = jnp.where(here0, place0, -1.0)
    near_ref[1:2, :] = jnp.where(here1, place1, -1.0)
    far_ref[0:1, :] = jnp.where(here0, -1.0, place0)
    far_ref[1:2, :] = jnp.where(here1, -1.0, place1)
    near_ref[2:4, :] = gate_ref[...]
    far_ref[2:4, :] = gate_ref[...]

    def back_in(ids, slot):
        return (((ids >> 2) * 2 + (ids & 1)) * 2 * CAP).astype(F32) + slot

    back0, back1 = back_in(ids0, slot0), back_in(ids1, slot1)
    near_ref[4:5, :] = jnp.where(here0, back0, -1.0)
    near_ref[5:6, :] = jnp.where(here1, back1, -1.0)
    far_ref[4:5, :] = jnp.where(here0, -1.0, back0 + CAP)
    far_ref[5:6, :] = jnp.where(here1, -1.0, back1 + CAP)
    near_ref[6:8, :] = gate_ref[...]
    far_ref[6:8, :] = gate_ref[...]


def fill_tokens(column_ref, chosen, tok_ref, out_ref):
    for i in range(8):
        source = pl.multiple_of(column_ref[i] * 256, 256)
        out_ref[:, i * 256 : (i + 1) * 256] = jnp.dot(
            chosen, tok_ref[:, pl.ds(source, 256)], preferred_element_type=F32
        ).astype(BF16)


def fill_grads(first, second, chosen, aux_ref, grad_ref, out_ref, at):
    for i in range(8):
        out_ref[:, at + i * 256 : at + (i + 1) * 256] = jnp.dot(
            chosen, grad_ref[:, i * 256 : (i + 1) * 256], preferred_element_type=F32
        ).astype(BF16)
    gate = jnp.sum(
        jnp.where(first, aux_ref[2:3, :], 0.0) + jnp.where(second, aux_ref[3:4, :], 0.0),
        axis=1,
        keepdims=True,
    )
    out_ref[:, at + WIDTH :] = jnp.broadcast_to(gate, (HALF_SLOTS, EXTRA)).astype(BF16)


def spread_kernel(column_ref, aux_ref, tok_ref, grad_ref, out_ref):
    first, second = one_hots(aux_ref)
    chosen = as_bf16(first | second)
    fill_tokens(column_ref, chosen, tok_ref, out_ref)
    fill_grads(first, second, chosen, aux_ref, grad_ref, out_ref, WIDTH)


def spread_tokens_kernel(column_ref, aux_ref, tok_ref, out_ref):
    first, second = one_hots(aux_ref)
    fill_tokens(column_ref, as_bf16(first | second), tok_ref, out_ref)


def spread_grads_kernel(aux_ref, grad_ref, out_ref):
    first, second = one_hots(aux_ref)
    fill_grads(first, second, as_bf16(first | second), aux_ref, grad_ref, out_ref, 0)


def collect_kernel(near_aux_ref, far_aux_ref, rows_ref, near_ref, far_ref):
    to_tokens = (((0,), (0,)), ((), ()))
    number = lax.broadcasted_iota(jnp.int32, (SLOTS, TOK), 0)
    for aux_ref, out_ref in ((near_aux_ref, near_ref), (far_aux_ref, far_ref)):
        pos = aux_ref[4:6, :].astype(jnp.int32)
        first, second = number == pos[0:1, :], number == pos[1:2, :]
        out_ref[:, :WIDTH] = lax.dot_general(
            as_bf16(first | second),
            rows_ref[:, :WIDTH],
            to_tokens,
            preferred_element_type=F32,
        ).astype(out_ref.dtype)
        score = rows_ref[:, WIDTH:]
        score0 = lax.dot_general(as_bf16(first), score, to_tokens, preferred_element_type=F32)
        score1 = lax.dot_general(as_bf16(second), score, to_tokens, preferred_element_type=F32)
        lane = lax.broadcasted_iota(jnp.int32, (TOK, EXTRA), 1)
        out_ref[:, WIDTH:] = jnp.where(lane == 0, score0, score1).astype(out_ref.dtype)


def finish_kernel(column_ref, near_ref, far_ref, out_ref, score_ref):
    for i in range(8):
        target = pl.multiple_of(column_ref[i] * 256, 256)
        part = slice(i * 256, (i + 1) * 256)
        out_ref[:, pl.ds(target, 256)] = (near_ref[:, part] + far_ref[:, part].astype(F32)).astype(
            BF16
        )
    score_ref[...] = (near_ref[:, WIDTH:] + far_ref[:, WIDTH:].astype(F32)).astype(BF16)


HIDDEN = 768
SCALE_IN = WIDTH ** (-0.5)
SCALE_OUT = HIDDEN ** (-0.5)
BOTH = (slice(0, HALF_SLOTS), slice(HALF_SLOTS, SLOTS))
TN = (((0,), (0,)), ((), ()))
NT = (((1,), (1,)), ((), ()))


def dot(a, b, dims=(((1,), (0,)), ((), ()))):
    return lax.dot_general(a, b, dims, preferred_element_type=F32)


def pack_down(down):
    tail = [down[32 * j : 32 * j + 32, 1536:] for j in range(3)]
    return jnp.concatenate([down[:, :1536], jnp.concatenate(tail, axis=1)], axis=0)


def unpack_down(packed):
    tail = [packed[96:128, 512 * j : 512 * j + 512] for j in range(3)]
    return jnp.concatenate([packed[:96], jnp.concatenate(tail, axis=0)], axis=1)


def shard_parts(refs):
    own, other, below, above, up2, down2, up3, down3 = refs
    return [
        ((own, 0), (own, 192)),
        ((other, 0), (other, 192)),
        ((above, 0), (above, 192)),
        ((down2, 0), (down2, 192)),
        ((up3, 0), (down3, 0)),
        ((up3, 192), (down3, 192)),
        ((below, 0), (below, 192)),
        ((up2, 0), (up2, 192)),
    ]


def gate_up_parts(refs):
    return [[(ref, at, 128) for ref, at in halves] for halves in shard_parts(refs)]


def down_parts(refs):
    return [[(ref, at + 128, 64) for ref, at in halves] for halves in shard_parts(refs)]


def read(pieces, columns):
    got = [ref[at : at + rows, columns] for ref, at, rows in pieces]
    return got[0] if len(got) == 1 else jnp.concatenate(got, axis=0)


def forward_kernel(column_ref, near_ref, far_ref, *refs):
    weights, (act_ref, slope_ref, swish_ref, down_ref) = refs[:8], refs[8:]
    blocks = gate_up_parts(weights)
    for rows, x_ref in zip(BOTH, (near_ref, far_ref)):
        for f in range(3):
            lo = slice(f * 256, f * 256 + 256)
            hi = slice(HIDDEN + f * 256, HIDDEN + f * 256 + 256)
            gate = jnp.zeros((HALF_SLOTS, 256), F32)
            up = jnp.zeros((HALF_SLOTS, 256), F32)
            for i, pieces in enumerate(blocks):
                x = x_ref[:, i * 256 : i * 256 + 256]
                gate += dot(x, read(pieces, lo))
                up += dot(x, read(pieces, hi))
            gate = gate * SCALE_IN
            up = up * SCALE_IN
            sig = jax.nn.sigmoid(gate)
            swish = gate * sig
            act_ref[rows, lo] = (swish * up).astype(BF16)
            slope_ref[rows, lo] = (up * sig * (1.0 + gate * (1.0 - sig))).astype(BF16)
            swish_ref[rows, lo] = swish.astype(BF16)
    for i, pieces in enumerate(down_parts(weights)):
        row = pl.multiple_of(column_ref[i] * 96, 32)
        packed = read(pieces, slice(None))
        down_ref[pl.ds(row, 96), :1536] = packed[:96]
        for j in range(3):
            down_ref[pl.ds(row + 32 * j, 32), 1536:] = packed[96:128, 512 * j : 512 * j + 512]


def backward_kernel(
    near_ref,
    far_in_ref,
    far_grad_ref,
    slope_ref,
    swish_ref,
    down_ref,
    proj_ref,
    far_plane_ref,
    scaled_ref,
):
    for rows, grad_ref, at in ((BOTH[0], near_ref, WIDTH), (BOTH[1], far_grad_ref, 0)):
        gate = grad_ref[:, at + WIDTH : at + WIDTH + EXTRA].astype(F32)
        gate = gate[:, 0:1]
        for n in range(4):
            grad = grad_ref[:, at + n * 512 : at + n * 512 + 512].astype(F32)
            scaled_ref[rows, n * 512 : n * 512 + 512] = (gate * grad).astype(BF16)
    for rows in BOTH:
        for f in range(3):
            lo = slice(f * 256, f * 256 + 256)
            grad_act = SCALE_OUT * dot(scaled_ref[rows, :], down_ref[lo, :], NT)
            proj_ref[rows, lo] = (grad_act * slope_ref[rows, lo].astype(F32)).astype(BF16)
            proj_ref[rows, HIDDEN + f * 256 : HIDDEN + f * 256 + 256] = (
                grad_act * swish_ref[rows, lo].astype(F32)
            ).astype(BF16)
    plane_product(near_ref, far_in_ref, proj_ref, far_plane_ref, 2)


def parts_kernel(column_ref, act_ref, scaled_ref, parts_ref, whole_ref):
    for n in range(4):
        part = slice(n * 512, n * 512 + 512)
        for f in range(3):
            lo = slice(f * 256, f * 256 + 256)
            whole_ref[lo, part] = (SCALE_OUT * dot(act_ref[:, lo], scaled_ref[:, part], TN)).astype(
                BF16
            )
    for i in range(8):
        row = pl.multiple_of(column_ref[i] * 96, 32)
        parts_ref[i, 0:96, :] = whole_ref[pl.ds(row, 96), :1536]
        for j in range(3):
            parts_ref[i, 96:128, 512 * j : 512 * j + 512] = whole_ref[
                pl.ds(row + 32 * j, 32), 1536:
            ]


def plane_product(near_ref, far_ref, proj_ref, out_ref, k):
    for half in range(2):
        at = k * 512 + half * 256
        for n in range(3):
            part = slice(n * 512, n * 512 + 512)
            total = dot(near_ref[:, at : at + 256], proj_ref[BOTH[0], part], TN)
            total += dot(far_ref[:, at : at + 256], proj_ref[BOTH[1], part], TN)
            out_ref[half * 256 : half * 256 + 256, part] = (SCALE_IN * total).astype(BF16)


def planes_kernel(near_ref, far_ref, proj_ref, above_ref, below_ref):
    plane_product(near_ref, far_ref, proj_ref, above_ref, 1)
    plane_product(near_ref, far_ref, proj_ref, below_ref, 3)


def own_plane_kernel(near_ref, far_ref, proj_ref, own_ref):
    plane_product(near_ref, far_ref, proj_ref, own_ref, 0)


def back_kernel(near_ref, far_grad_ref, act_ref, proj_ref, down_ref, *refs):
    blocks, out_ref = gate_up_parts(refs[:8]), refs[8]
    for which, (rows, grad_ref, at) in enumerate(
        ((BOTH[0], near_ref, WIDTH), (BOTH[1], far_grad_ref, 0))
    ):

        def store(columns, value):
            value = value.astype(BF16)
            for i in range(8):
                out_ref[i * 96 + which * 48 : i * 96 + which * 48 + 48, columns] = value[
                    i * 48 : i * 48 + 48
                ]

        for i, pieces in enumerate(blocks):
            route = SCALE_IN * dot(proj_ref[rows, :], read(pieces, slice(None)), NT)
            store(slice(i * 256, i * 256 + 256), route)
        score = jnp.zeros((HALF_SLOTS, 1), F32)
        for n in range(8):
            part = slice(n * 256, n * 256 + 256)
            out = SCALE_OUT * dot(act_ref[rows, :], down_ref[:, part])
            grad = grad_ref[:, at + n * 256 : at + n * 256 + 256].astype(F32)
            score += jnp.sum(grad * out, axis=1, keepdims=True)
        store(slice(WIDTH, WIDTH + EXTRA), jnp.broadcast_to(score, (HALF_SLOTS, EXTRA)))


def add(*refs_or_values):
    total = refs_or_values[0].astype(F32)
    for value in refs_or_values[1:]:
        total = total + value.astype(F32)
    return total


def copy_all(pairs, sems):
    copies = [
        pltpu.make_async_copy(source, target, sems.at[i]) for i, (source, target) in enumerate(pairs)
    ]
    for copy in copies:
        copy.start()
    for copy in copies:
        copy.wait()


def pass_on_kernel(below_ref, above_ref, up2_ref, down2_ref, up_ref, down_ref, sems):
    copy_all(
        [
            (below_ref.at[0:192], up_ref.at[0:192]),
            (above_ref.at[192:384], down_ref.at[0:192]),
            (up2_ref.at[0:192], up_ref.at[192:384]),
            (down2_ref.at[192:384], down_ref.at[192:384]),
        ],
        sems,
    )


def pass_on(below, above, up2, down2):
    vmem = pl.BlockSpec(memory_space=pltpu.VMEM)
    return pl.pallas_call(
        pass_on_kernel,
        out_shape=(bf(384, 1536), bf(384, 1536)),
        in_specs=[pl.BlockSpec(memory_space=pl.ANY)] * 4,
        out_specs=(vmem, vmem),
        scratch_shapes=[pltpu.SemaphoreType.DMA((4,))],
        cost_estimate=pl.CostEstimate(flops=0, bytes_accessed=4_800_000, transcendentals=0),
        compiler_params=pltpu.CompilerParams(vmem_limit_bytes=6 << 20),
    )(below, above, up2, down2)


def place_kernel(pieces, column_ref, *refs):
    gu_ref, dn_ref, sems = refs[-3:]
    pairs = []
    for block, (first, first_at), (last, last_at) in pieces:
        row = pl.multiple_of(column_ref[block] * 256, 256)
        pairs.append((refs[first].at[pl.ds(first_at, 128)], gu_ref.at[pl.ds(row, 128)]))
        pairs.append((refs[last].at[pl.ds(last_at, 128)], gu_ref.at[pl.ds(row + 128, 128)]))
        row = pl.multiple_of(column_ref[block] * 96, 32)
        first_at, last_at = first_at + 128, last_at + 128
        main = pl.ds(0, 1536)
        pairs.append((refs[first].at[pl.ds(first_at, 64)], dn_ref.at[pl.ds(row, 64), main]))
        pairs.append((refs[last].at[pl.ds(last_at, 32)], dn_ref.at[pl.ds(row + 64, 32), main]))
        for j in range(3):
            tail = refs[last].at[pl.ds(last_at + 32, 32), pl.ds(512 * j, 512)]
            pairs.append((tail, dn_ref.at[pl.ds(row + 32 * j, 32), pl.ds(1536, 512)]))
    copy_all(pairs, sems)


def place_shards(columns, shards, pieces, whole=()):
    anywhere = pl.BlockSpec(memory_space=pl.ANY)
    vmem = pl.BlockSpec(memory_space=pltpu.VMEM)
    given = len(shards)
    return pl.pallas_call(
        functools.partial(place_kernel, pieces),
        out_shape=(bf(8 * 256, 1536), bf(8 * 96, WIDTH)),
        in_specs=[pl.BlockSpec(memory_space=pltpu.SMEM)] + [vmem] * given + [anywhere] * len(whole),
        out_specs=(anywhere, anywhere),
        scratch_shapes=[pltpu.SemaphoreType.DMA((7 * len(pieces),))],
        input_output_aliases={given + 1: 0, given + 2: 1} if whole else {},
        cost_estimate=pl.CostEstimate(
            flops=0, bytes_accessed=2_400_000 * len(pieces), transcendentals=0
        ),
        compiler_params=pltpu.CompilerParams(vmem_limit_bytes=16 << 20),
    )(columns, *shards, *whole)


def second_kernel(far_ref, above_ref, below_ref, parts_ref, up_ref, down_ref, y_ref, o_up, o_down):
    o_up[0:128] = add(above_ref[256:384], up_ref[...]).astype(BF16)
    o_up[128:256] = above_ref[384:512]
    o_up[256:384] = far_ref[0:128]
    o_up[384:448] = add(parts_ref[4, 0:64], y_ref[0:64]).astype(BF16)
    o_down[0:128] = below_ref[256:384]
    o_down[128:256] = add(below_ref[384:512], down_ref[...]).astype(BF16)
    o_down[256:384] = far_ref[128:256]
    o_down[384:448] = add(parts_ref[4, 64:128], y_ref[64:128]).astype(BF16)


def third_kernel(
    above_ref, below_ref, own_ref, parts_ref, up_ref, down_ref, y_ref, o_up, o_down, o_y
):
    o_up[0:128] = add(above_ref[0:128], up_ref[256:384]).astype(BF16)
    o_up[128:256] = above_ref[128:256]
    o_up[256:320] = add(parts_ref[2, 0:64], y_ref[0:64], up_ref[384:448]).astype(BF16)
    o_up[320:384] = add(parts_ref[2, 64:128], y_ref[64:128]).astype(BF16)
    o_down[0:128] = below_ref[0:128]
    o_down[128:256] = add(below_ref[128:256], down_ref[256:384]).astype(BF16)
    o_down[256:320] = add(parts_ref[6, 0:64], y_ref[128:192]).astype(BF16)
    o_down[320:384] = add(parts_ref[6, 64:128], y_ref[192:256], down_ref[384:448]).astype(BF16)
    o_y[0:256] = add(own_ref[256:512], up_ref[0:256], down_ref[0:256]).astype(BF16)
    o_y[256:384] = parts_ref[1]


def update_kernel(
    own_ref, parts_ref, up_ref, down_ref, y_ref, w_gu, m_gu, s_gu, w_dn, m_dn, s_dn, w_tail, m_tail,
    s_tail, out_ref
):
    grad = add(own_ref[...], up_ref[0:256], down_ref[0:256], y_ref[0:256])
    new = adam_update(w_gu[...], m_gu[...], s_gu[...], grad)[0].astype(BF16)
    out_ref[0:128] = new[:128]
    out_ref[192:320] = new[128:]
    grad = add(parts_ref[0], up_ref[256:384], down_ref[256:384], y_ref[256:384])
    new = adam_update(w_dn[...], m_dn[...], s_dn[...], grad[:96])[0].astype(BF16)
    out_ref[128:192] = new[:64]
    out_ref[320:352] = new[64:]
    new = adam_update(w_tail[...], m_tail[...], s_tail[...], grad[96:])[0].astype(BF16)
    out_ref[352:384] = new


def update_call(own_plane, parts, t_up, t_down, t_y, state):
    gu = pl.BlockSpec((256, 512), lambda c: (0, c))
    packed = pl.BlockSpec((384, 512), lambda c: (0, c))
    part = pl.BlockSpec((1, 128, 512), lambda c: (0, 0, c))
    dn = pl.BlockSpec((96, 512), lambda c: (0, c))
    tail = pl.BlockSpec((32, 512), lambda c: (c, 3))
    w_gu, w_dn, m_gu, m_dn, s_gu, s_dn = state
    return pl.pallas_call(
        update_kernel,
        out_shape=bf(384, 1536),
        grid=(3,),
        in_specs=[gu, part, packed, packed, packed] + [gu] * 3 + [dn] * 3 + [tail] * 3,
        out_specs=packed,
        cost_estimate=pl.CostEstimate(
            flops=20_000_000, bytes_accessed=12_000_000, transcendentals=1_000_000
        ),
        compiler_params=pltpu.CompilerParams(vmem_limit_bytes=48 << 20),
    )(own_plane, parts, t_up, t_down, t_y, w_gu, m_gu, s_gu, w_dn, m_dn, s_dn, w_dn, m_dn, s_dn)


def tie(*arrays):
    return lax.optimization_barrier(arrays)


def bf(*shape):
    return jax.ShapeDtypeStruct(shape, BF16)


def f32(*shape):
    return jax.ShapeDtypeStruct(shape, F32)


def call(kernel, outs, inputs, scalars=0, scratch=(), flops=0):
    vmem = pl.BlockSpec(memory_space=pltpu.VMEM)
    smem = pl.BlockSpec(memory_space=pltpu.SMEM)
    moved = sum(a.size * a.dtype.itemsize for a in inputs) + sum(
        o.size * o.dtype.itemsize for o in outs
    )
    held = sum(math.prod(s.shape) * 2 for s in scratch)
    got = pl.pallas_call(
        kernel,
        out_shape=outs,
        in_specs=[smem] * scalars + [vmem] * (len(inputs) - scalars),
        out_specs=(vmem,) * len(outs),
        scratch_shapes=scratch,
        cost_estimate=pl.CostEstimate(flops=flops, bytes_accessed=moved, transcendentals=0),
        compiler_params=pltpu.CompilerParams(vmem_limit_bytes=moved + held + (3 << 20)),
    )(*inputs)
    return got if len(outs) > 1 else got[0]


def local(
    tokens,
    out_grad,
    expert_ids,
    gate_values,
    master_gate_up,
    master_down,
    moment_gate_up,
    moment_down,
    second_gate_up,
    second_down,
):
    r = lax.axis_index("dp")
    z, y = r // 2, r % 2
    order = [(k, dy) for k in range(4) for dy in range(2)]
    columns = jnp.stack([((z + k) % 4) * 2 + (y ^ dy) for k, dy in order])
    half = ((lax.axis_index("expert") >> 1) & 1).reshape(1)

    gu = master_gate_up[0].astype(BF16)
    dn = pack_down(master_down[0].astype(BF16))
    own = jnp.concatenate([gu[:128], dn[:64], gu[128:], dn[64:]], axis=0)
    below, above, other = z_up(own), z_down(own), y_swap(own)
    near_aux, far_aux = call(
        route_kernel,
        (f32(8, TOK), f32(8, TOK)),
        (half, expert_ids.T, gate_values.astype(F32).T),
        scalars=1,
    )
    near = call(
        spread_kernel,
        (bf(HALF_SLOTS, 2 * WIDTH + EXTRA),),
        (columns, near_aux, tokens, out_grad),
        scalars=1,
    )
    below, above, other, far_aux, near, tok_next, grad_next = tie(
        below, above, other, far_aux, near, tokens, out_grad
    )

    up2, down2 = z_up(other), z_down(other)
    their_aux, their_tok = yh_swap(far_aux), yh_swap(tok_next)
    near = exchange(near)
    up2, down2, their_aux, their_tok, grad_next = tie(
        up2, down2, their_aux, their_tok, grad_next
    )

    up3, down3 = pass_on(below, above, up2, down2)
    up3, down3, their_grad = z_up(up3), z_down(down3), yh_swap(grad_next)
    send_far = call(
        spread_tokens_kernel,
        (bf(HALF_SLOTS, WIDTH),),
        (columns, their_aux, their_tok),
        scalars=1,
    )
    send_far, near = tie(send_far, near)
    far_in = exchange(send_far)
    up3, down3, their_grad = tie(up3, down3, their_grad)
    send_far = call(spread_grads_kernel, (bf(HALF_SLOTS, WIDTH + EXTRA),), (their_aux, their_grad))
    send_far, far_in = tie(send_far, far_in)
    far_grad = exchange(send_far)
    weights = (own, other, below, above, up2, down2, up3, down3)

    act, slope, swish, down = call(
        forward_kernel,
        (
            bf(SLOTS, HIDDEN),
            bf(SLOTS, HIDDEN),
            bf(SLOTS, HIDDEN),
            bf(HIDDEN, WIDTH),
        ),
        (columns, near, far_in) + weights,
        scalars=1,
        flops=4_800_000_000,
    )
    proj, far_plane, scaled = call(
        backward_kernel,
        (bf(SLOTS, 2 * HIDDEN), bf(512, 1536), bf(SLOTS, WIDTH)),
        (near, far_in, far_grad, slope, swish, down),
        flops=3_600_000_000,
    )

    t_up = z_up(far_plane[256:384])
    t_down = z_down(far_plane[384:512])
    parts = call(
        parts_kernel,
        (bf(8, 128, 1536),),
        (columns, act, scaled),
        scalars=1,
        scratch=(pltpu.VMEM((HIDDEN, WIDTH), BF16),),
        flops=2_400_000_000,
    )
    t_y = y_swap(parts[5])
    above_plane, below_plane = call(
        planes_kernel,
        (bf(512, 1536),) * 2,
        (near, far_in, proj),
        flops=2_400_000_000,
    )
    t_up, t_down, t_y, above_plane, below_plane, late_proj = tie(
        t_up, t_down, t_y, above_plane, below_plane, proj
    )
    s_up, s_down = call(
        second_kernel,
        (bf(448, 1536), bf(448, 1536)),
        (far_plane, above_plane, below_plane, parts, t_up, t_down, t_y),
    )
    s_y = jnp.concatenate([parts[3], parts[7]], axis=0)
    t_up, t_down, t_y = z_up(s_up), z_down(s_down), y_swap(s_y)
    own_plane = call(
        own_plane_kernel, (bf(512, 1536),), (near, far_in, late_proj), flops=1_200_000_000
    )
    back = call(
        back_kernel,
        (bf(SLOTS, WIDTH + EXTRA),),
        (near, far_grad, act, late_proj, down) + weights,
        flops=7_200_000_000,
    )
    t_up, t_down, t_y, back, own_plane = tie(t_up, t_down, t_y, back, own_plane)
    s_up, s_down, s_y = call(
        third_kernel,
        (bf(384, 1536),) * 3,
        (above_plane, below_plane, own_plane, parts, t_up, t_down, t_y),
    )
    t_up, t_down, t_y = z_up(s_up), z_down(s_down), y_swap(s_y)
    returned = exchange(back)
    t_up, t_down, t_y = tie(t_up, t_down, t_y)
    state = (
        master_gate_up[0],
        master_down[0],
        moment_gate_up[0],
        moment_down[0],
        second_gate_up[0],
        second_down[0],
    )
    new_own = update_call(own_plane, parts, t_up, t_down, t_y, state)

    below, above, other = z_up(new_own), z_down(new_own), y_swap(new_own)
    grad_gate_up = add(own_plane[:256], t_up[:256], t_down[:256], t_y[:256])
    grad_down = unpack_down(add(parts[0], t_up[256:], t_down[256:], t_y[256:]))
    master_gu_next, moment_gu_next, second_gu_next = adam_update(
        state[0], state[2], state[4], grad_gate_up
    )
    master_dn_next, moment_dn_next, second_dn_next = adam_update(
        state[1], state[3], state[5], grad_down
    )
    near_sum, far_sum = call(
        collect_kernel,
        (f32(TOK, WIDTH + EXTRA), bf(TOK, WIDTH + EXTRA)),
        (near_aux, their_aux, returned),
        flops=1_700_000_000,
    )
    below, above, other, far_sum, *kept = tie(
        below,
        above,
        other,
        far_sum,
        master_gu_next,
        moment_gu_next,
        second_gu_next,
        master_dn_next,
        moment_dn_next,
        second_dn_next,
    )
    (
        master_gu_next,
        moment_gu_next,
        second_gu_next,
        master_dn_next,
        moment_dn_next,
        second_dn_next,
    ) = kept
    up2, down2 = z_up(other), z_down(other)
    far_sum = yh_swap(far_sum)

    pieces = [(i, (n, 0), (n, 192)) for n, i in enumerate((0, 1, 2, 6))]
    new_gate_up, new_down = place_shards(columns, (new_own, other, above, below), pieces)
    up2, down2, far_sum, new_gate_up, new_down = tie(up2, down2, far_sum, new_gate_up, new_down)
    up3, down3 = pass_on(below, above, up2, down2)
    up3, down3 = z_up(up3), z_down(down3)
    new_gate_up, new_down = place_shards(
        columns,
        (down2, up2),
        [(3, (0, 0), (0, 192)), (7, (1, 0), (1, 192))],
        (new_gate_up, new_down),
    )
    input_grad, scores = call(
        finish_kernel,
        (bf(TOK, WIDTH), bf(TOK, EXTRA)),
        (columns, near_sum, far_sum),
        scalars=1,
    )
    up3, down3, new_gate_up, new_down, input_grad = tie(
        up3, down3, new_gate_up, new_down, input_grad
    )
    new_gate_up, new_down = place_shards(
        columns,
        (up3, down3),
        [(4, (0, 0), (1, 0)), (5, (0, 192), (1, 192))],
        (new_gate_up, new_down),
    )
    gate_grad = scores[:, :2]
    return (
        input_grad,
        gate_grad,
        new_gate_up[None],
        new_down[None],
        master_gu_next[None],
        master_dn_next[None],
        moment_gu_next[None],
        moment_dn_next[None],
        second_gu_next[None],
        second_dn_next[None],
    )


def solution(mesh):
    rows = P(("dp", "expert"), None)
    state = P("expert", "dp", None)
    whole = P("expert", None, None)
    return jax.shard_map(
        local,
        mesh=mesh,
        in_specs=(rows,) * 4 + (state,) * 6,
        out_specs=(rows, rows, whole, whole) + (state,) * 6,
        check_vma=False,
    )
```

```python
import functools
import math

import jax
import jax.numpy as jnp
from jax import lax
from jax.experimental import pallas as pl
from jax.experimental.pallas import tpu as pltpu
from jax.sharding import PartitionSpec as P

beta_first = 0.9
beta_second = 0.95
learn_rate = 0.01
weight_decay = 0.1
adam_epsilon = 1e-08
bias_first = 0.9999734386
bias_second = 0.9940794708

F32 = jnp.float32
BF16 = jnp.bfloat16

Z_UP = [(i, (i + 2) % 8) for i in range(8)]
Z_DOWN = [(i, (i - 2) % 8) for i in range(8)]
Y_SWAP = [(i, i ^ 1) for i in range(8)]


def z_up(a):
    return lax.ppermute(a, "dp", Z_UP)


def z_down(a):
    return lax.ppermute(a, "dp", Z_DOWN)


def y_swap(a):
    return lax.ppermute(a, "dp", Y_SWAP)


def adam_update(master, moment, second, grad):
    moment_next = beta_first * moment + (1.0 - beta_first) * grad
    second_next = beta_second * second + (1.0 - beta_second) * grad * grad
    step_size = moment_next / bias_first / (jnp.sqrt(second_next / bias_second) + adam_epsilon)
    master_next = master - learn_rate * (step_size + weight_decay * master)
    return (master_next, moment_next, second_next)


CAP = 48
HALF_SLOTS = 8 * CAP
SLOTS = 16 * CAP
TOK = 256
WIDTH = 2048
EXTRA = 128
YH_SWAP = [(i, i ^ 2) for i in range(16)]
X_GROUPS = [[x * 4 + h * 2 + c for x in range(4) for c in range(2)] for h in range(2)]


def yh_swap(a):
    return lax.ppermute(a, "expert", YH_SWAP)


def exchange(rows):
    return lax.all_to_all(
        rows.reshape(8, rows.shape[0] // 8, rows.shape[1]),
        "expert",
        split_axis=0,
        concat_axis=0,
        axis_index_groups=X_GROUPS,
        tiled=True,
    ).reshape(rows.shape)


def one_hots(aux_ref):
    number = lax.broadcasted_iota(jnp.int32, (HALF_SLOTS, TOK), 0)
    pos = aux_ref[0:2, :].astype(jnp.int32)
    return number == pos[0:1, :], number == pos[1:2, :]


def as_bf16(mask):
    return mask.astype(F32).astype(BF16)


def route_kernel(half_ref, ids_ref, gate_ref, near_ref, far_ref):
    ids0, ids1 = ids_ref[0:1, :], ids_ref[1:2, :]
    expert = lax.broadcasted_iota(jnp.int32, (16, TOK), 0)
    hit0 = expert == ids0
    hit1 = expert == ids1
    ahead = as_bf16(
        lax.broadcasted_iota(jnp.int32, (TOK, TOK), 0)
        < lax.broadcasted_iota(jnp.int32, (TOK, TOK), 1)
    )
    one0 = hit0.astype(F32)
    before0 = jnp.dot(as_bf16(hit0), ahead, preferred_element_type=F32)
    before1 = jnp.dot(as_bf16(hit1), ahead, preferred_element_type=F32)
    before1 = before1 + jnp.sum(one0, axis=1, keepdims=True)
    slot0 = jnp.sum(jnp.where(hit0, before0, 0.0), axis=0, keepdims=True)
    slot1 = jnp.sum(jnp.where(hit1, before1, 0.0), axis=0, keepdims=True)

    def place_in(ids, slot):
        return (((ids >> 2) * 2 + (ids & 1)) * CAP).astype(F32) + slot

    place0, place1 = place_in(ids0, slot0), place_in(ids1, slot1)
    here0 = ((ids0 >> 1) & 1) == half_ref[0]
    here1 = ((ids1 >> 1) & 1) == half_ref[0]
    near_ref[0:1, :] = jnp.where(here0, place0, -1.0)
    near_ref[1:2, :] = jnp.where(here1, place1, -1.0)
    far_ref[0:1, :] = jnp.where(here0, -1.0, place0)
    far_ref[1:2, :] = jnp.where(here1, -1.0, place1)
    near_ref[2:4, :] = gate_ref[...]
    far_ref[2:4, :] = gate_ref[...]

    def back_in(ids, slot):
        return (((ids >> 2) * 2 + (ids & 1)) * 2 * CAP).astype(F32) + slot

    back0, back1 = back_in(ids0, slot0), back_in(ids1, slot1)
    near_ref[4:5, :] = jnp.where(here0, back0, -1.0)
    near_ref[5:6, :] = jnp.where(here1, back1, -1.0)
    far_ref[4:5, :] = jnp.where(here0, -1.0, back0 + CAP)
    far_ref[5:6, :] = jnp.where(here1, -1.0, back1 + CAP)
    near_ref[6:8, :] = gate_ref[...]
    far_ref[6:8, :] = gate_ref[...]


def fill_tokens(column_ref, chosen, tok_ref, out_ref):
    for i in range(8):
        source = pl.multiple_of(column_ref[i] * 256, 256)
        out_ref[:, i * 256 : (i + 1) * 256] = jnp.dot(
            chosen, tok_ref[:, pl.ds(source, 256)], preferred_element_type=F32
        ).astype(BF16)


def fill_grads(first, second, chosen, aux_ref, grad_ref, out_ref, at):
    for i in range(8):
        out_ref[:, at + i * 256 : at + (i + 1) * 256] = jnp.dot(
            chosen, grad_ref[:, i * 256 : (i + 1) * 256], preferred_element_type=F32
        ).astype(BF16)
    gate = jnp.sum(
        jnp.where(first, aux_ref[2:3, :], 0.0) + jnp.where(second, aux_ref[3:4, :], 0.0),
        axis=1,
        keepdims=True,
    )
    out_ref[:, at + WIDTH :] = jnp.broadcast_to(gate, (HALF_SLOTS, EXTRA)).astype(BF16)


def spread_kernel(column_ref, aux_ref, tok_ref, grad_ref, out_ref):
    first, second = one_hots(aux_ref)
    chosen = as_bf16(first | second)
    fill_tokens(column_ref, chosen, tok_ref, out_ref)
    fill_grads(first, second, chosen, aux_ref, grad_ref, out_ref, WIDTH)


def spread_tokens_kernel(column_ref, aux_ref, tok_ref, out_ref):
    first, second = one_hots(aux_ref)
    fill_tokens(column_ref, as_bf16(first | second), tok_ref, out_ref)


def spread_grads_kernel(aux_ref, grad_ref, out_ref):
    first, second = one_hots(aux_ref)
    fill_grads(first, second, as_bf16(first | second), aux_ref, grad_ref, out_ref, 0)


def collect_kernel(near_aux_ref, far_aux_ref, rows_ref, near_ref, far_ref):
    to_tokens = (((0,), (0,)), ((), ()))
    number = lax.broadcasted_iota(jnp.int32, (SLOTS, TOK), 0)
    for aux_ref, out_ref in ((near_aux_ref, near_ref), (far_aux_ref, far_ref)):
        pos = aux_ref[4:6, :].astype(jnp.int32)
        first, second = number == pos[0:1, :], number == pos[1:2, :]
        out_ref[:, :WIDTH] = lax.dot_general(
            as_bf16(first | second),
            rows_ref[:, :WIDTH],
            to_tokens,
            preferred_element_type=F32,
        ).astype(out_ref.dtype)
        score = rows_ref[:, WIDTH:]
        score0 = lax.dot_general(as_bf16(first), score, to_tokens, preferred_element_type=F32)
        score1 = lax.dot_general(as_bf16(second), score, to_tokens, preferred_element_type=F32)
        lane = lax.broadcasted_iota(jnp.int32, (TOK, EXTRA), 1)
        out_ref[:, WIDTH:] = jnp.where(lane == 0, score0, score1).astype(out_ref.dtype)


def finish_kernel(column_ref, near_ref, far_ref, out_ref, score_ref):
    for i in range(8):
        target = pl.multiple_of(column_ref[i] * 256, 256)
        part = slice(i * 256, (i + 1) * 256)
        out_ref[:, pl.ds(target, 256)] = (near_ref[:, part] + far_ref[:, part].astype(F32)).astype(
            BF16
        )
    score_ref[...] = (near_ref[:, WIDTH:] + far_ref[:, WIDTH:].astype(F32)).astype(BF16)


HIDDEN = 768
SCALE_IN = WIDTH ** (-0.5)
SCALE_OUT = HIDDEN ** (-0.5)
BOTH = (slice(0, HALF_SLOTS), slice(HALF_SLOTS, SLOTS))
TN = (((0,), (0,)), ((), ()))
NT = (((1,), (1,)), ((), ()))


def dot(a, b, dims=(((1,), (0,)), ((), ()))):
    return lax.dot_general(a, b, dims, preferred_element_type=F32)


def pack_down(down):
    tail = [down[32 * j : 32 * j + 32, 1536:] for j in range(3)]
    return jnp.concatenate([down[:, :1536], jnp.concatenate(tail, axis=1)], axis=0)


def unpack_down(packed):
    tail = [packed[96:128, 512 * j : 512 * j + 512] for j in range(3)]
    return jnp.concatenate([packed[:96], jnp.concatenate(tail, axis=0)], axis=1)


def shard_parts(refs):
    own, other, below, above, up2, down2, up3, down3 = refs
    return [
        ((own, 0), (own, 192)),
        ((other, 0), (other, 192)),
        ((above, 0), (above, 192)),
        ((down2, 0), (down2, 192)),
        ((up3, 0), (down3, 0)),
        ((up3, 192), (down3, 192)),
        ((below, 0), (below, 192)),
        ((up2, 0), (up2, 192)),
    ]


def gate_up_parts(refs):
    return [[(ref, at, 128) for ref, at in halves] for halves in shard_parts(refs)]


def down_parts(refs):
    return [[(ref, at + 128, 64) for ref, at in halves] for halves in shard_parts(refs)]


def read(pieces, columns):
    got = [ref[at : at + rows, columns] for ref, at, rows in pieces]
    return got[0] if len(got) == 1 else jnp.concatenate(got, axis=0)


def forward_kernel(column_ref, near_ref, far_ref, *refs):
    weights, (act_ref, slope_ref, swish_ref, down_ref) = refs[:8], refs[8:]
    blocks = gate_up_parts(weights)
    for rows, x_ref in zip(BOTH, (near_ref, far_ref)):
        for f in range(3):
            lo = slice(f * 256, f * 256 + 256)
            hi = slice(HIDDEN + f * 256, HIDDEN + f * 256 + 256)
            gate = jnp.zeros((HALF_SLOTS, 256), F32)
            up = jnp.zeros((HALF_SLOTS, 256), F32)
            for i, pieces in enumerate(blocks):
                x = x_ref[:, i * 256 : i * 256 + 256]
                gate += dot(x, read(pieces, lo))
                up += dot(x, read(pieces, hi))
            gate = gate * SCALE_IN
            up = up * SCALE_IN
            sig = jax.nn.sigmoid(gate)
            swish = gate * sig
            act_ref[rows, lo] = (swish * up).astype(BF16)
            slope_ref[rows, lo] = (up * sig * (1.0 + gate * (1.0 - sig))).astype(BF16)
            swish_ref[rows, lo] = swish.astype(BF16)
    for i, pieces in enumerate(down_parts(weights)):
        row = pl.multiple_of(column_ref[i] * 96, 32)
        packed = read(pieces, slice(None))
        down_ref[pl.ds(row, 96), :1536] = packed[:96]
        for j in range(3):
            down_ref[pl.ds(row + 32 * j, 32), 1536:] = packed[96:128, 512 * j : 512 * j + 512]


def backward_kernel(
    near_ref,
    far_in_ref,
    far_grad_ref,
    slope_ref,
    swish_ref,
    down_ref,
    proj_ref,
    far_plane_ref,
    scaled_ref,
):
    for rows, grad_ref, at in ((BOTH[0], near_ref, WIDTH), (BOTH[1], far_grad_ref, 0)):
        gate = grad_ref[:, at + WIDTH : at + WIDTH + EXTRA].astype(F32)
        gate = gate[:, 0:1]
        for n in range(4):
            grad = grad_ref[:, at + n * 512 : at + n * 512 + 512].astype(F32)
            scaled_ref[rows, n * 512 : n * 512 + 512] = (gate * grad).astype(BF16)
    for rows in BOTH:
        for f in range(3):
            lo = slice(f * 256, f * 256 + 256)
            grad_act = SCALE_OUT * dot(scaled_ref[rows, :], down_ref[lo, :], NT)
            proj_ref[rows, lo] = (grad_act * slope_ref[rows, lo].astype(F32)).astype(BF16)
            proj_ref[rows, HIDDEN + f * 256 : HIDDEN + f * 256 + 256] = (
                grad_act * swish_ref[rows, lo].astype(F32)
            ).astype(BF16)
    plane_product(near_ref, far_in_ref, proj_ref, far_plane_ref, 2)


def parts_kernel(column_ref, act_ref, scaled_ref, parts_ref, whole_ref):
    for n in range(4):
        part = slice(n * 512, n * 512 + 512)
        for f in range(3):
            lo = slice(f * 256, f * 256 + 256)
            whole_ref[lo, part] = (SCALE_OUT * dot(act_ref[:, lo], scaled_ref[:, part], TN)).astype(
                BF16
            )
    for i in range(8):
        row = pl.multiple_of(column_ref[i] * 96, 32)
        parts_ref[i, 0:96, :] = whole_ref[pl.ds(row, 96), :1536]
        for j in range(3):
            parts_ref[i, 96:128, 512 * j : 512 * j + 512] = whole_ref[
                pl.ds(row + 32 * j, 32), 1536:
            ]


def plane_product(near_ref, far_ref, proj_ref, out_ref, k):
    for half in range(2):
        at = k * 512 + half * 256
        for n in range(3):
            part = slice(n * 512, n * 512 + 512)
            total = dot(near_ref[:, at : at + 256], proj_ref[BOTH[0], part], TN)
            total += dot(far_ref[:, at : at + 256], proj_ref[BOTH[1], part], TN)
            out_ref[half * 256 : half * 256 + 256, part] = (SCALE_IN * total).astype(BF16)


def planes_kernel(near_ref, far_ref, proj_ref, above_ref, below_ref):
    plane_product(near_ref, far_ref, proj_ref, above_ref, 1)
    plane_product(near_ref, far_ref, proj_ref, below_ref, 3)


def own_plane_kernel(near_ref, far_ref, proj_ref, own_ref):
    plane_product(near_ref, far_ref, proj_ref, own_ref, 0)


def back_kernel(near_ref, far_grad_ref, act_ref, proj_ref, down_ref, *refs):
    blocks, out_ref = gate_up_parts(refs[:8]), refs[8]
    for which, (rows, grad_ref, at) in enumerate(
        ((BOTH[0], near_ref, WIDTH), (BOTH[1], far_grad_ref, 0))
    ):

        def store(columns, value):
            value = value.astype(BF16)
            for i in range(8):
                out_ref[i * 96 + which * 48 : i * 96 + which * 48 + 48, columns] = value[
                    i * 48 : i * 48 + 48
                ]

        for i, pieces in enumerate(blocks):
            route = SCALE_IN * dot(proj_ref[rows, :], read(pieces, slice(None)), NT)
            store(slice(i * 256, i * 256 + 256), route)
        score = jnp.zeros((HALF_SLOTS, 1), F32)
        for n in range(8):
            part = slice(n * 256, n * 256 + 256)
            out = SCALE_OUT * dot(act_ref[rows, :], down_ref[:, part])
            grad = grad_ref[:, at + n * 256 : at + n * 256 + 256].astype(F32)
            score += jnp.sum(grad * out, axis=1, keepdims=True)
        store(slice(WIDTH, WIDTH + EXTRA), jnp.broadcast_to(score, (HALF_SLOTS, EXTRA)))


def add(*refs_or_values):
    total = refs_or_values[0].astype(F32)
    for value in refs_or_values[1:]:
        total = total + value.astype(F32)
    return total


def copy_all(pairs, sems):
    copies = [
        pltpu.make_async_copy(source, target, sems.at[i]) for i, (source, target) in enumerate(pairs)
    ]
    for copy in copies:
        copy.start()
    for copy in copies:
        copy.wait()


def pass_on_kernel(below_ref, above_ref, up2_ref, down2_ref, up_ref, down_ref, sems):
    copy_all(
        [
            (below_ref.at[0:192], up_ref.at[0:192]),
            (above_ref.at[192:384], down_ref.at[0:192]),
            (up2_ref.at[0:192], up_ref.at[192:384]),
            (down2_ref.at[192:384], down_ref.at[192:384]),
        ],
        sems,
    )


def pass_on(below, above, up2, down2, grant):
    vmem = pl.BlockSpec(memory_space=pltpu.VMEM)
    return pl.pallas_call(
        pass_on_kernel,
        out_shape=(bf(384, 1536), bf(384, 1536)),
        in_specs=[pl.BlockSpec(memory_space=pl.ANY)] * 4,
        out_specs=(vmem, vmem),
        scratch_shapes=[pltpu.SemaphoreType.DMA((4,))],
        cost_estimate=pl.CostEstimate(flops=0, bytes_accessed=4_800_000, transcendentals=0),
        compiler_params=pltpu.CompilerParams(vmem_limit_bytes=grant),
    )(below, above, up2, down2)


def place_kernel(pieces, column_ref, *refs):
    gu_ref, dn_ref, sems = refs[-3:]
    pairs = []
    for block, (first, first_at), (last, last_at) in pieces:
        row = pl.multiple_of(column_ref[block] * 256, 256)
        pairs.append((refs[first].at[pl.ds(first_at, 128)], gu_ref.at[pl.ds(row, 128)]))
        pairs.append((refs[last].at[pl.ds(last_at, 128)], gu_ref.at[pl.ds(row + 128, 128)]))
        row = pl.multiple_of(column_ref[block] * 96, 32)
        first_at, last_at = first_at + 128, last_at + 128
        main = pl.ds(0, 1536)
        pairs.append((refs[first].at[pl.ds(first_at, 64)], dn_ref.at[pl.ds(row, 64), main]))
        pairs.append((refs[last].at[pl.ds(last_at, 32)], dn_ref.at[pl.ds(row + 64, 32), main]))
        for j in range(3):
            tail = refs[last].at[pl.ds(last_at + 32, 32), pl.ds(512 * j, 512)]
            pairs.append((tail, dn_ref.at[pl.ds(row + 32 * j, 32), pl.ds(1536, 512)]))
    copy_all(pairs, sems)


def place_shards(columns, shards, pieces, whole=()):
    anywhere = pl.BlockSpec(memory_space=pl.ANY)
    vmem = pl.BlockSpec(memory_space=pltpu.VMEM)
    given = len(shards)
    return pl.pallas_call(
        functools.partial(place_kernel, pieces),
        out_shape=(bf(8 * 256, 1536), bf(8 * 96, WIDTH)),
        in_specs=[pl.BlockSpec(memory_space=pltpu.SMEM)] + [vmem] * given + [anywhere] * len(whole),
        out_specs=(anywhere, anywhere),
        scratch_shapes=[pltpu.SemaphoreType.DMA((7 * len(pieces),))],
        input_output_aliases={given + 1: 0, given + 2: 1} if whole else {},
        cost_estimate=pl.CostEstimate(
            flops=0, bytes_accessed=2_400_000 * len(pieces), transcendentals=0
        ),
        compiler_params=pltpu.CompilerParams(vmem_limit_bytes=16 << 20),
    )(columns, *shards, *whole)


def second_kernel(far_ref, above_ref, below_ref, parts_ref, up_ref, down_ref, y_ref, o_up, o_down):
    o_up[0:128] = add(above_ref[256:384], up_ref[...]).astype(BF16)
    o_up[128:256] = above_ref[384:512]
    o_up[256:384] = far_ref[0:128]
    o_up[384:448] = add(parts_ref[4, 0:64], y_ref[0:64]).astype(BF16)
    o_down[0:128] = below_ref[256:384]
    o_down[128:256] = add(below_ref[384:512], down_ref[...]).astype(BF16)
    o_down[256:384] = far_ref[128:256]
    o_down[384:448] = add(parts_ref[4, 64:128], y_ref[64:128]).astype(BF16)


def third_kernel(
    above_ref, below_ref, own_ref, parts_ref, up_ref, down_ref, y_ref, o_up, o_down, o_y
):
    o_up[0:128] = add(above_ref[0:128], up_ref[256:384]).astype(BF16)
    o_up[128:256] = above_ref[128:256]
    o_up[256:320] = add(parts_ref[2, 0:64], y_ref[0:64], up_ref[384:448]).astype(BF16)
    o_up[320:384] = add(parts_ref[2, 64:128], y_ref[64:128]).astype(BF16)
    o_down[0:128] = below_ref[0:128]
    o_down[128:256] = add(below_ref[128:256], down_ref[256:384]).astype(BF16)
    o_down[256:320] = add(parts_ref[6, 0:64], y_ref[128:192]).astype(BF16)
    o_down[320:384] = add(parts_ref[6, 64:128], y_ref[192:256], down_ref[384:448]).astype(BF16)
    o_y[0:256] = add(own_ref[256:512], up_ref[0:256], down_ref[0:256]).astype(BF16)
    o_y[256:384] = parts_ref[1]


def update_kernel(
    own_ref, parts_ref, up_ref, down_ref, y_ref, w_gu, m_gu, s_gu, w_dn, m_dn, s_dn, w_tail, m_tail,
    s_tail, out_ref
):
    grad = add(own_ref[...], up_ref[0:256], down_ref[0:256], y_ref[0:256])
    new = adam_update(w_gu[...], m_gu[...], s_gu[...], grad)[0].astype(BF16)
    out_ref[0:128] = new[:128]
    out_ref[192:320] = new[128:]
    grad = add(parts_ref[0], up_ref[256:384], down_ref[256:384], y_ref[256:384])
    new = adam_update(w_dn[...], m_dn[...], s_dn[...], grad[:96])[0].astype(BF16)
    out_ref[128:192] = new[:64]
    out_ref[320:352] = new[64:]
    new = adam_update(w_tail[...], m_tail[...], s_tail[...], grad[96:])[0].astype(BF16)
    out_ref[352:384] = new


def update_call(own_plane, parts, t_up, t_down, t_y, state):
    gu = pl.BlockSpec((256, 512), lambda c: (0, c))
    packed = pl.BlockSpec((384, 512), lambda c: (0, c))
    part = pl.BlockSpec((1, 128, 512), lambda c: (0, 0, c))
    dn = pl.BlockSpec((96, 512), lambda c: (0, c))
    tail = pl.BlockSpec((32, 512), lambda c: (c, 3))
    w_gu, w_dn, m_gu, m_dn, s_gu, s_dn = state
    return pl.pallas_call(
        update_kernel,
        out_shape=bf(384, 1536),
        grid=(3,),
        in_specs=[gu, part, packed, packed, packed] + [gu] * 3 + [dn] * 3 + [tail] * 3,
        out_specs=packed,
        cost_estimate=pl.CostEstimate(
            flops=20_000_000, bytes_accessed=12_000_000, transcendentals=1_000_000
        ),
        compiler_params=pltpu.CompilerParams(vmem_limit_bytes=48 << 20),
    )(own_plane, parts, t_up, t_down, t_y, w_gu, m_gu, s_gu, w_dn, m_dn, s_dn, w_dn, m_dn, s_dn)


def tie(*arrays):
    return lax.optimization_barrier(arrays)


def bf(*shape):
    return jax.ShapeDtypeStruct(shape, BF16)


def f32(*shape):
    return jax.ShapeDtypeStruct(shape, F32)


def call(kernel, outs, inputs, scalars=0, scratch=(), flops=0):
    vmem = pl.BlockSpec(memory_space=pltpu.VMEM)
    smem = pl.BlockSpec(memory_space=pltpu.SMEM)
    moved = sum(a.size * a.dtype.itemsize for a in inputs) + sum(
        o.size * o.dtype.itemsize for o in outs
    )
    held = sum(math.prod(s.shape) * 2 for s in scratch)
    got = pl.pallas_call(
        kernel,
        out_shape=outs,
        in_specs=[smem] * scalars + [vmem] * (len(inputs) - scalars),
        out_specs=(vmem,) * len(outs),
        scratch_shapes=scratch,
        cost_estimate=pl.CostEstimate(flops=flops, bytes_accessed=moved, transcendentals=0),
        compiler_params=pltpu.CompilerParams(vmem_limit_bytes=moved + held + (3 << 20)),
    )(*inputs)
    return got if len(outs) > 1 else got[0]


def local(
    tokens,
    out_grad,
    expert_ids,
    gate_values,
    master_gate_up,
    master_down,
    moment_gate_up,
    moment_down,
    second_gate_up,
    second_down,
):
    r = lax.axis_index("dp")
    z, y = r // 2, r % 2
    order = [(k, dy) for k in range(4) for dy in range(2)]
    columns = jnp.stack([((z + k) % 4) * 2 + (y ^ dy) for k, dy in order])
    half = ((lax.axis_index("expert") >> 1) & 1).reshape(1)

    gu = master_gate_up[0].astype(BF16)
    dn = pack_down(master_down[0].astype(BF16))
    own = jnp.concatenate([gu[:128], dn[:64], gu[128:], dn[64:]], axis=0)
    below, above, other = z_up(own), z_down(own), y_swap(own)
    near_aux, far_aux = call(
        route_kernel,
        (f32(8, TOK), f32(8, TOK)),
        (half, expert_ids.T, gate_values.astype(F32).T),
        scalars=1,
    )
    near = call(
        spread_kernel,
        (bf(HALF_SLOTS, 2 * WIDTH + EXTRA),),
        (columns, near_aux, tokens, out_grad),
        scalars=1,
    )
    below, above, other, far_aux, near, tok_next, grad_next = tie(
        below, above, other, far_aux, near, tokens, out_grad
    )

    up2, down2 = z_up(other), z_down(other)
    their_aux, their_tok = yh_swap(far_aux), yh_swap(tok_next)
    near = exchange(near)
    up2, down2, their_aux, their_tok, grad_next = tie(
        up2, down2, their_aux, their_tok, grad_next
    )

    up3, down3 = pass_on(below, above, up2, down2, 56 << 20)
    up3, down3, their_grad = z_up(up3), z_down(down3), yh_swap(grad_next)
    send_far = call(
        spread_tokens_kernel,
        (bf(HALF_SLOTS, WIDTH),),
        (columns, their_aux, their_tok),
        scalars=1,
    )
    send_far, near = tie(send_far, near)
    far_in = exchange(send_far)
    up3, down3, their_grad = tie(up3, down3, their_grad)
    send_far = call(spread_grads_kernel, (bf(HALF_SLOTS, WIDTH + EXTRA),), (their_aux, their_grad))
    send_far, far_in = tie(send_far, far_in)
    far_grad = exchange(send_far)
    weights = (own, other, below, above, up2, down2, up3, down3)

    act, slope, swish, down = call(
        forward_kernel,
        (
            bf(SLOTS, HIDDEN),
            bf(SLOTS, HIDDEN),
            bf(SLOTS, HIDDEN),
            bf(HIDDEN, WIDTH),
        ),
        (columns, near, far_in) + weights,
        scalars=1,
        flops=4_800_000_000,
    )
    proj, far_plane, scaled = call(
        backward_kernel,
        (bf(SLOTS, 2 * HIDDEN), bf(512, 1536), bf(SLOTS, WIDTH)),
        (near, far_in, far_grad, slope, swish, down),
        flops=3_600_000_000,
    )

    t_up = z_up(far_plane[256:384])
    t_down = z_down(far_plane[384:512])
    parts = call(
        parts_kernel,
        (bf(8, 128, 1536),),
        (columns, act, scaled),
        scalars=1,
        scratch=(pltpu.VMEM((HIDDEN, WIDTH), BF16),),
        flops=2_400_000_000,
    )
    t_y = y_swap(parts[5])
    above_plane, below_plane = call(
        planes_kernel,
        (bf(512, 1536),) * 2,
        (near, far_in, proj),
        flops=2_400_000_000,
    )
    t_up, t_down, t_y, above_plane, below_plane, late_proj = tie(
        t_up, t_down, t_y, above_plane, below_plane, proj
    )
    s_up, s_down = call(
        second_kernel,
        (bf(448, 1536), bf(448, 1536)),
        (far_plane, above_plane, below_plane, parts, t_up, t_down, t_y),
    )
    s_y = jnp.concatenate([parts[3], parts[7]], axis=0)
    t_up, t_down, t_y = z_up(s_up), z_down(s_down), y_swap(s_y)
    own_plane = call(
        own_plane_kernel, (bf(512, 1536),), (near, far_in, late_proj), flops=1_200_000_000
    )
    back = call(
        back_kernel,
        (bf(SLOTS, WIDTH + EXTRA),),
        (near, far_grad, act, late_proj, down) + weights,
        flops=7_200_000_000,
    )
    t_up, t_down, t_y, back, own_plane = tie(t_up, t_down, t_y, back, own_plane)
    s_up, s_down, s_y = call(
        third_kernel,
        (bf(384, 1536),) * 3,
        (above_plane, below_plane, own_plane, parts, t_up, t_down, t_y),
    )
    t_up, t_down, t_y = z_up(s_up), z_down(s_down), y_swap(s_y)
    returned = exchange(back)
    t_up, t_down, t_y = tie(t_up, t_down, t_y)
    state = (
        master_gate_up[0],
        master_down[0],
        moment_gate_up[0],
        moment_down[0],
        second_gate_up[0],
        second_down[0],
    )
    new_own = update_call(own_plane, parts, t_up, t_down, t_y, state)

    below, above, other = z_up(new_own), z_down(new_own), y_swap(new_own)
    grad_gate_up = add(own_plane[:256], t_up[:256], t_down[:256], t_y[:256])
    grad_down = unpack_down(add(parts[0], t_up[256:], t_down[256:], t_y[256:]))
    master_gu_next, moment_gu_next, second_gu_next = adam_update(
        state[0], state[2], state[4], grad_gate_up
    )
    master_dn_next, moment_dn_next, second_dn_next = adam_update(
        state[1], state[3], state[5], grad_down
    )
    near_sum, far_sum = call(
        collect_kernel,
        (f32(TOK, WIDTH + EXTRA), bf(TOK, WIDTH + EXTRA)),
        (near_aux, their_aux, returned),
        flops=1_700_000_000,
    )
    below, above, other, far_sum, *kept = tie(
        below,
        above,
        other,
        far_sum,
        master_gu_next,
        moment_gu_next,
        second_gu_next,
        master_dn_next,
        moment_dn_next,
        second_dn_next,
    )
    (
        master_gu_next,
        moment_gu_next,
        second_gu_next,
        master_dn_next,
        moment_dn_next,
        second_dn_next,
    ) = kept
    up2, down2 = z_up(other), z_down(other)
    far_sum = yh_swap(far_sum)

    pieces = [(i, (n, 0), (n, 192)) for n, i in enumerate((0, 1, 2, 6))]
    new_gate_up, new_down = place_shards(columns, (new_own, other, above, below), pieces)
    up2, down2, far_sum, new_gate_up, new_down = tie(up2, down2, far_sum, new_gate_up, new_down)
    up3, down3 = pass_on(below, above, up2, down2, 6 << 20)
    up3, down3 = z_up(up3), z_down(down3)
    new_gate_up, new_down = place_shards(
        columns,
        (down2, up2),
        [(3, (0, 0), (0, 192)), (7, (1, 0), (1, 192))],
        (new_gate_up, new_down),
    )
    input_grad, scores = call(
        finish_kernel,
        (bf(TOK, WIDTH), bf(TOK, EXTRA)),
        (columns, near_sum, far_sum),
        scalars=1,
    )
    up3, down3, new_gate_up, new_down, input_grad = tie(
        up3, down3, new_gate_up, new_down, input_grad
    )
    new_gate_up, new_down = place_shards(
        columns,
        (up3, down3),
        [(4, (0, 0), (1, 0)), (5, (0, 192), (1, 192))],
        (new_gate_up, new_down),
    )
    gate_grad = scores[:, :2]
    return (
        input_grad,
        gate_grad,
        new_gate_up[None],
        new_down[None],
        master_gu_next[None],
        master_dn_next[None],
        moment_gu_next[None],
        moment_dn_next[None],
        second_gu_next[None],
        second_dn_next[None],
    )


def solution(mesh):
    rows = P(("dp", "expert"), None)
    state = P("expert", "dp", None)
    whole = P("expert", None, None)
    return jax.shard_map(
        local,
        mesh=mesh,
        in_specs=(rows,) * 4 + (state,) * 6,
        out_specs=(rows, rows, whole, whole) + (state,) * 6,
        check_vma=False,
    )
```

```python
import functools
import math

import jax
import jax.numpy as jnp
from jax import lax
from jax.experimental import pallas as pl
from jax.experimental.pallas import tpu as pltpu
from jax.sharding import PartitionSpec as P

beta_first = 0.9
beta_second = 0.95
learn_rate = 0.01
weight_decay = 0.1
adam_epsilon = 1e-08
bias_first = 0.9999734386
bias_second = 0.9940794708

F32 = jnp.float32
BF16 = jnp.bfloat16

Z_UP = [(i, (i + 2) % 8) for i in range(8)]
Z_DOWN = [(i, (i - 2) % 8) for i in range(8)]
Y_SWAP = [(i, i ^ 1) for i in range(8)]


def z_up(a):
    return lax.ppermute(a, "dp", Z_UP)


def z_down(a):
    return lax.ppermute(a, "dp", Z_DOWN)


def y_swap(a):
    return lax.ppermute(a, "dp", Y_SWAP)


def adam_update(master, moment, second, grad):
    moment_next = beta_first * moment + (1.0 - beta_first) * grad
    second_next = beta_second * second + (1.0 - beta_second) * grad * grad
    step_size = moment_next / bias_first / (jnp.sqrt(second_next / bias_second) + adam_epsilon)
    master_next = master - learn_rate * (step_size + weight_decay * master)
    return (master_next, moment_next, second_next)


CAP = 48
HALF_SLOTS = 8 * CAP
SLOTS = 16 * CAP
TOK = 256
WIDTH = 2048
EXTRA = 128
YH_SWAP = [(i, i ^ 2) for i in range(16)]
X_GROUPS = [[x * 4 + h * 2 + c for x in range(4) for c in range(2)] for h in range(2)]


def yh_swap(a):
    return lax.ppermute(a, "expert", YH_SWAP)


def exchange(rows):
    return lax.all_to_all(
        rows.reshape(8, rows.shape[0] // 8, rows.shape[1]),
        "expert",
        split_axis=0,
        concat_axis=0,
        axis_index_groups=X_GROUPS,
        tiled=True,
    ).reshape(rows.shape)


def one_hots(aux_ref):
    number = lax.broadcasted_iota(jnp.int32, (HALF_SLOTS, TOK), 0)
    pos = aux_ref[0:2, :].astype(jnp.int32)
    return number == pos[0:1, :], number == pos[1:2, :]


def as_bf16(mask):
    return mask.astype(F32).astype(BF16)


def route_kernel(half_ref, ids_ref, gate_ref, near_ref, far_ref):
    ids0, ids1 = ids_ref[0:1, :], ids_ref[1:2, :]
    expert = lax.broadcasted_iota(jnp.int32, (16, TOK), 0)
    hit0 = expert == ids0
    hit1 = expert == ids1
    ahead = as_bf16(
        lax.broadcasted_iota(jnp.int32, (TOK, TOK), 0)
        < lax.broadcasted_iota(jnp.int32, (TOK, TOK), 1)
    )
    one0 = hit0.astype(F32)
    before0 = jnp.dot(as_bf16(hit0), ahead, preferred_element_type=F32)
    before1 = jnp.dot(as_bf16(hit1), ahead, preferred_element_type=F32)
    before1 = before1 + jnp.sum(one0, axis=1, keepdims=True)
    slot0 = jnp.sum(jnp.where(hit0, before0, 0.0), axis=0, keepdims=True)
    slot1 = jnp.sum(jnp.where(hit1, before1, 0.0), axis=0, keepdims=True)

    def place_in(ids, slot):
        return (((ids >> 2) * 2 + (ids & 1)) * CAP).astype(F32) + slot

    place0, place1 = place_in(ids0, slot0), place_in(ids1, slot1)
    here0 = ((ids0 >> 1) & 1) == half_ref[0]
    here1 = ((ids1 >> 1) & 1) == half_ref[0]
    near_ref[0:1, :] = jnp.where(here0, place0, -1.0)
    near_ref[1:2, :] = jnp.where(here1, place1, -1.0)
    far_ref[0:1, :] = jnp.where(here0, -1.0, place0)
    far_ref[1:2, :] = jnp.where(here1, -1.0, place1)
    near_ref[2:4, :] = gate_ref[...]
    far_ref[2:4, :] = gate_ref[...]

    def back_in(ids, slot):
        return (((ids >> 2) * 2 + (ids & 1)) * 2 * CAP).astype(F32) + slot

    back0, back1 = back_in(ids0, slot0), back_in(ids1, slot1)
    near_ref[4:5, :] = jnp.where(here0, back0, -1.0)
    near_ref[5:6, :] = jnp.where(here1, back1, -1.0)
    far_ref[4:5, :] = jnp.where(here0, -1.0, back0 + CAP)
    far_ref[5:6, :] = jnp.where(here1, -1.0, back1 + CAP)
    near_ref[6:8, :] = gate_ref[...]
    far_ref[6:8, :] = gate_ref[...]


def fill_tokens(column_ref, chosen, tok_ref, out_ref):
    for i in range(8):
        source = pl.multiple_of(column_ref[i] * 256, 256)
        out_ref[:, i * 256 : (i + 1) * 256] = jnp.dot(
            chosen, tok_ref[:, pl.ds(source, 256)], preferred_element_type=F32
        ).astype(BF16)


def fill_grads(first, second, chosen, aux_ref, grad_ref, out_ref, at):
    for i in range(8):
        out_ref[:, at + i * 256 : at + (i + 1) * 256] = jnp.dot(
            chosen, grad_ref[:, i * 256 : (i + 1) * 256], preferred_element_type=F32
        ).astype(BF16)
    gate = jnp.sum(
        jnp.where(first, aux_ref[2:3, :], 0.0) + jnp.where(second, aux_ref[3:4, :], 0.0),
        axis=1,
        keepdims=True,
    )
    out_ref[:, at + WIDTH :] = jnp.broadcast_to(gate, (HALF_SLOTS, EXTRA)).astype(BF16)


def spread_kernel(column_ref, aux_ref, tok_ref, grad_ref, out_ref):
    first, second = one_hots(aux_ref)
    chosen = as_bf16(first | second)
    fill_tokens(column_ref, chosen, tok_ref, out_ref)
    fill_grads(first, second, chosen, aux_ref, grad_ref, out_ref, WIDTH)


def spread_tokens_kernel(column_ref, aux_ref, tok_ref, out_ref):
    first, second = one_hots(aux_ref)
    fill_tokens(column_ref, as_bf16(first | second), tok_ref, out_ref)


def spread_grads_kernel(aux_ref, grad_ref, out_ref):
    first, second = one_hots(aux_ref)
    fill_grads(first, second, as_bf16(first | second), aux_ref, grad_ref, out_ref, 0)


def collect_kernel(near_aux_ref, far_aux_ref, rows_ref, near_ref, far_ref):
    to_tokens = (((0,), (0,)), ((), ()))
    number = lax.broadcasted_iota(jnp.int32, (SLOTS, TOK), 0)
    for aux_ref, out_ref in ((near_aux_ref, near_ref), (far_aux_ref, far_ref)):
        pos = aux_ref[4:6, :].astype(jnp.int32)
        first, second = number == pos[0:1, :], number == pos[1:2, :]
        out_ref[:, :WIDTH] = lax.dot_general(
            as_bf16(first | second),
            rows_ref[:, :WIDTH],
            to_tokens,
            preferred_element_type=F32,
        ).astype(out_ref.dtype)
        score = rows_ref[:, WIDTH:]
        score0 = lax.dot_general(as_bf16(first), score, to_tokens, preferred_element_type=F32)
        score1 = lax.dot_general(as_bf16(second), score, to_tokens, preferred_element_type=F32)
        lane = lax.broadcasted_iota(jnp.int32, (TOK, EXTRA), 1)
        out_ref[:, WIDTH:] = jnp.where(lane == 0, score0, score1).astype(out_ref.dtype)


def finish_kernel(column_ref, near_ref, far_ref, out_ref, score_ref):
    for i in range(8):
        target = pl.multiple_of(column_ref[i] * 256, 256)
        part = slice(i * 256, (i + 1) * 256)
        out_ref[:, pl.ds(target, 256)] = (near_ref[:, part] + far_ref[:, part].astype(F32)).astype(
            BF16
        )
    score_ref[...] = (near_ref[:, WIDTH:] + far_ref[:, WIDTH:].astype(F32)).astype(BF16)


HIDDEN = 768
SCALE_IN = WIDTH ** (-0.5)
SCALE_OUT = HIDDEN ** (-0.5)
BOTH = (slice(0, HALF_SLOTS), slice(HALF_SLOTS, SLOTS))
TN = (((0,), (0,)), ((), ()))
NT = (((1,), (1,)), ((), ()))


def dot(a, b, dims=(((1,), (0,)), ((), ()))):
    return lax.dot_general(a, b, dims, preferred_element_type=F32)


def pack_down(down):
    tail = [down[32 * j : 32 * j + 32, 1536:] for j in range(3)]
    return jnp.concatenate([down[:, :1536], jnp.concatenate(tail, axis=1)], axis=0)


def unpack_down(packed):
    tail = [packed[96:128, 512 * j : 512 * j + 512] for j in range(3)]
    return jnp.concatenate([packed[:96], jnp.concatenate(tail, axis=0)], axis=1)


def shard_parts(refs):
    own, other, below, above, up2, down2, up3, down3 = refs
    return [
        ((own, 0), (own, 192)),
        ((other, 0), (other, 192)),
        ((above, 0), (above, 192)),
        ((down2, 0), (down2, 192)),
        ((up3, 0), (down3, 0)),
        ((up3, 192), (down3, 192)),
        ((below, 0), (below, 192)),
        ((up2, 0), (up2, 192)),
    ]


def gate_up_parts(refs):
    return [[(ref, at, 128) for ref, at in halves] for halves in shard_parts(refs)]


def down_parts(refs):
    return [[(ref, at + 128, 64) for ref, at in halves] for halves in shard_parts(refs)]


def read(pieces, columns):
    got = [ref[at : at + rows, columns] for ref, at, rows in pieces]
    return got[0] if len(got) == 1 else jnp.concatenate(got, axis=0)


def forward_kernel(column_ref, near_ref, far_ref, *refs):
    weights, (act_ref, slope_ref, swish_ref, down_ref) = refs[:8], refs[8:]
    blocks = gate_up_parts(weights)
    for rows, x_ref in zip(BOTH, (near_ref, far_ref)):
        for f in range(3):
            lo = slice(f * 256, f * 256 + 256)
            hi = slice(HIDDEN + f * 256, HIDDEN + f * 256 + 256)
            gate = jnp.zeros((HALF_SLOTS, 256), F32)
            up = jnp.zeros((HALF_SLOTS, 256), F32)
            for i, pieces in enumerate(blocks):
                x = x_ref[:, i * 256 : i * 256 + 256]
                gate += dot(x, read(pieces, lo))
                up += dot(x, read(pieces, hi))
            gate = gate * SCALE_IN
            up = up * SCALE_IN
            sig = jax.nn.sigmoid(gate)
            swish = gate * sig
            act_ref[rows, lo] = (swish * up).astype(BF16)
            slope_ref[rows, lo] = (up * sig * (1.0 + gate * (1.0 - sig))).astype(BF16)
            swish_ref[rows, lo] = swish.astype(BF16)
    for i, pieces in enumerate(down_parts(weights)):
        row = pl.multiple_of(column_ref[i] * 96, 32)
        packed = read(pieces, slice(None))
        down_ref[pl.ds(row, 96), :1536] = packed[:96]
        for j in range(3):
            down_ref[pl.ds(row + 32 * j, 32), 1536:] = packed[96:128, 512 * j : 512 * j + 512]


def backward_kernel(
    near_ref,
    far_in_ref,
    far_grad_ref,
    slope_ref,
    swish_ref,
    down_ref,
    proj_ref,
    far_plane_ref,
    scaled_ref,
):
    for rows, grad_ref, at in ((BOTH[0], near_ref, WIDTH), (BOTH[1], far_grad_ref, 0)):
        gate = grad_ref[:, at + WIDTH : at + WIDTH + EXTRA].astype(F32)
        gate = gate[:, 0:1]
        for n in range(4):
            grad = grad_ref[:, at + n * 512 : at + n * 512 + 512].astype(F32)
            scaled_ref[rows, n * 512 : n * 512 + 512] = (gate * grad).astype(BF16)
    for rows in BOTH:
        for f in range(3):
            lo = slice(f * 256, f * 256 + 256)
            grad_act = SCALE_OUT * dot(scaled_ref[rows, :], down_ref[lo, :], NT)
            proj_ref[rows, lo] = (grad_act * slope_ref[rows, lo].astype(F32)).astype(BF16)
            proj_ref[rows, HIDDEN + f * 256 : HIDDEN + f * 256 + 256] = (
                grad_act * swish_ref[rows, lo].astype(F32)
            ).astype(BF16)
    plane_product(near_ref, far_in_ref, proj_ref, far_plane_ref, 2)


def parts_kernel(column_ref, act_ref, scaled_ref, parts_ref, whole_ref):
    for n in range(4):
        part = slice(n * 512, n * 512 + 512)
        for f in range(3):
            lo = slice(f * 256, f * 256 + 256)
            whole_ref[lo, part] = (SCALE_OUT * dot(act_ref[:, lo], scaled_ref[:, part], TN)).astype(
                BF16
            )
    for i in range(8):
        row = pl.multiple_of(column_ref[i] * 96, 32)
        parts_ref[i, 0:96, :] = whole_ref[pl.ds(row, 96), :1536]
        for j in range(3):
            parts_ref[i, 96:128, 512 * j : 512 * j + 512] = whole_ref[
                pl.ds(row + 32 * j, 32), 1536:
            ]


def plane_product(near_ref, far_ref, proj_ref, out_ref, k):
    for half in range(2):
        at = k * 512 + half * 256
        for n in range(3):
            part = slice(n * 512, n * 512 + 512)
            total = dot(near_ref[:, at : at + 256], proj_ref[BOTH[0], part], TN)
            total += dot(far_ref[:, at : at + 256], proj_ref[BOTH[1], part], TN)
            out_ref[half * 256 : half * 256 + 256, part] = (SCALE_IN * total).astype(BF16)


def planes_kernel(near_ref, far_ref, proj_ref, above_ref, below_ref):
    plane_product(near_ref, far_ref, proj_ref, above_ref, 1)
    plane_product(near_ref, far_ref, proj_ref, below_ref, 3)


def own_plane_kernel(near_ref, far_ref, proj_ref, own_ref):
    plane_product(near_ref, far_ref, proj_ref, own_ref, 0)


def back_kernel(near_ref, far_grad_ref, act_ref, proj_ref, down_ref, *refs):
    blocks, out_ref = gate_up_parts(refs[:8]), refs[8]
    for which, (rows, grad_ref, at) in enumerate(
        ((BOTH[0], near_ref, WIDTH), (BOTH[1], far_grad_ref, 0))
    ):

        def store(columns, value):
            value = value.astype(BF16)
            for i in range(8):
                out_ref[i * 96 + which * 48 : i * 96 + which * 48 + 48, columns] = value[
                    i * 48 : i * 48 + 48
                ]

        for i, pieces in enumerate(blocks):
            route = SCALE_IN * dot(proj_ref[rows, :], read(pieces, slice(None)), NT)
            store(slice(i * 256, i * 256 + 256), route)
        score = jnp.zeros((HALF_SLOTS, 1), F32)
        for n in range(8):
            part = slice(n * 256, n * 256 + 256)
            out = SCALE_OUT * dot(act_ref[rows, :], down_ref[:, part])
            grad = grad_ref[:, at + n * 256 : at + n * 256 + 256].astype(F32)
            score += jnp.sum(grad * out, axis=1, keepdims=True)
        store(slice(WIDTH, WIDTH + EXTRA), jnp.broadcast_to(score, (HALF_SLOTS, EXTRA)))


def add(*refs_or_values):
    total = refs_or_values[0].astype(F32)
    for value in refs_or_values[1:]:
        total = total + value.astype(F32)
    return total


def copy_all(pairs, sems):
    copies = [
        pltpu.make_async_copy(source, target, sems.at[i]) for i, (source, target) in enumerate(pairs)
    ]
    for copy in copies:
        copy.start()
    for copy in copies:
        copy.wait()


def pass_on_kernel(below_ref, above_ref, up2_ref, down2_ref, up_ref, down_ref, sems):
    copy_all(
        [
            (below_ref.at[0:192], up_ref.at[0:192]),
            (above_ref.at[192:384], down_ref.at[0:192]),
            (up2_ref.at[0:192], up_ref.at[192:384]),
            (down2_ref.at[192:384], down_ref.at[192:384]),
        ],
        sems,
    )


def pass_on(below, above, up2, down2, grant):
    vmem = pl.BlockSpec(memory_space=pltpu.VMEM)
    return pl.pallas_call(
        pass_on_kernel,
        out_shape=(bf(384, 1536), bf(384, 1536)),
        in_specs=[pl.BlockSpec(memory_space=pl.ANY)] * 4,
        out_specs=(vmem, vmem),
        scratch_shapes=[pltpu.SemaphoreType.DMA((4,))],
        cost_estimate=pl.CostEstimate(flops=0, bytes_accessed=4_800_000, transcendentals=0),
        compiler_params=pltpu.CompilerParams(vmem_limit_bytes=grant),
    )(below, above, up2, down2)


def place_kernel(pieces, column_ref, *refs):
    gu_ref, dn_ref, sems = refs[-3:]
    pairs = []
    for block, (first, first_at), (last, last_at) in pieces:
        row = pl.multiple_of(column_ref[block] * 256, 256)
        pairs.append((refs[first].at[pl.ds(first_at, 128)], gu_ref.at[pl.ds(row, 128)]))
        pairs.append((refs[last].at[pl.ds(last_at, 128)], gu_ref.at[pl.ds(row + 128, 128)]))
        row = pl.multiple_of(column_ref[block] * 96, 32)
        first_at, last_at = first_at + 128, last_at + 128
        main = pl.ds(0, 1536)
        pairs.append((refs[first].at[pl.ds(first_at, 64)], dn_ref.at[pl.ds(row, 64), main]))
        pairs.append((refs[last].at[pl.ds(last_at, 32)], dn_ref.at[pl.ds(row + 64, 32), main]))
        for j in range(3):
            tail = refs[last].at[pl.ds(last_at + 32, 32), pl.ds(512 * j, 512)]
            pairs.append((tail, dn_ref.at[pl.ds(row + 32 * j, 32), pl.ds(1536, 512)]))
    copy_all(pairs, sems)


def place_shards(columns, shards, pieces, whole=()):
    anywhere = pl.BlockSpec(memory_space=pl.ANY)
    vmem = pl.BlockSpec(memory_space=pltpu.VMEM)
    given = len(shards)
    return pl.pallas_call(
        functools.partial(place_kernel, pieces),
        out_shape=(bf(8 * 256, 1536), bf(8 * 96, WIDTH)),
        in_specs=[pl.BlockSpec(memory_space=pltpu.SMEM)] + [vmem] * given + [anywhere] * len(whole),
        out_specs=(anywhere, anywhere),
        scratch_shapes=[pltpu.SemaphoreType.DMA((7 * len(pieces),))],
        input_output_aliases={given + 1: 0, given + 2: 1} if whole else {},
        cost_estimate=pl.CostEstimate(
            flops=0, bytes_accessed=2_400_000 * len(pieces), transcendentals=0
        ),
        compiler_params=pltpu.CompilerParams(vmem_limit_bytes=16 << 20),
    )(columns, *shards, *whole)


def second_kernel(far_ref, above_ref, below_ref, parts_ref, up_ref, down_ref, y_ref, o_up, o_down):
    o_up[0:128] = add(above_ref[256:384], up_ref[...]).astype(BF16)
    o_up[128:256] = above_ref[384:512]
    o_up[256:384] = far_ref[0:128]
    o_up[384:448] = add(parts_ref[4, 0:64], y_ref[0:64]).astype(BF16)
    o_down[0:128] = below_ref[256:384]
    o_down[128:256] = add(below_ref[384:512], down_ref[...]).astype(BF16)
    o_down[256:384] = far_ref[128:256]
    o_down[384:448] = add(parts_ref[4, 64:128], y_ref[64:128]).astype(BF16)


def third_kernel(
    above_ref, below_ref, own_ref, parts_ref, up_ref, down_ref, y_ref, o_up, o_down, o_y
):
    o_up[0:128] = add(above_ref[0:128], up_ref[256:384]).astype(BF16)
    o_up[128:256] = above_ref[128:256]
    o_up[256:320] = add(parts_ref[2, 0:64], y_ref[0:64], up_ref[384:448]).astype(BF16)
    o_up[320:384] = add(parts_ref[2, 64:128], y_ref[64:128]).astype(BF16)
    o_down[0:128] = below_ref[0:128]
    o_down[128:256] = add(below_ref[128:256], down_ref[256:384]).astype(BF16)
    o_down[256:320] = add(parts_ref[6, 0:64], y_ref[128:192]).astype(BF16)
    o_down[320:384] = add(parts_ref[6, 64:128], y_ref[192:256], down_ref[384:448]).astype(BF16)
    o_y[0:256] = add(own_ref[256:512], up_ref[0:256], down_ref[0:256]).astype(BF16)
    o_y[256:384] = parts_ref[1]


def update_kernel(
    own_ref, parts_ref, up_ref, down_ref, y_ref, w_gu, m_gu, s_gu, w_dn, m_dn, s_dn, w_tail, m_tail,
    s_tail, out_ref
):
    grad = add(own_ref[...], up_ref[0:256], down_ref[0:256], y_ref[0:256])
    new = adam_update(w_gu[...], m_gu[...], s_gu[...], grad)[0].astype(BF16)
    out_ref[0:128] = new[:128]
    out_ref[192:320] = new[128:]
    grad = add(parts_ref[0], up_ref[256:384], down_ref[256:384], y_ref[256:384])
    new = adam_update(w_dn[...], m_dn[...], s_dn[...], grad[:96])[0].astype(BF16)
    out_ref[128:192] = new[:64]
    out_ref[320:352] = new[64:]
    new = adam_update(w_tail[...], m_tail[...], s_tail[...], grad[96:])[0].astype(BF16)
    out_ref[352:384] = new


def update_call(own_plane, parts, t_up, t_down, t_y, state):
    gu = pl.BlockSpec((256, 512), lambda c: (0, c))
    packed = pl.BlockSpec((384, 512), lambda c: (0, c))
    part = pl.BlockSpec((1, 128, 512), lambda c: (0, 0, c))
    dn = pl.BlockSpec((96, 512), lambda c: (0, c))
    tail = pl.BlockSpec((32, 512), lambda c: (c, 3))
    w_gu, w_dn, m_gu, m_dn, s_gu, s_dn = state
    return pl.pallas_call(
        update_kernel,
        out_shape=bf(384, 1536),
        grid=(3,),
        in_specs=[gu, part, packed, packed, packed] + [gu] * 3 + [dn] * 3 + [tail] * 3,
        out_specs=packed,
        cost_estimate=pl.CostEstimate(
            flops=20_000_000, bytes_accessed=12_000_000, transcendentals=1_000_000
        ),
        compiler_params=pltpu.CompilerParams(vmem_limit_bytes=24 << 20),
    )(own_plane, parts, t_up, t_down, t_y, w_gu, m_gu, s_gu, w_dn, m_dn, s_dn, w_dn, m_dn, s_dn)


def tie(*arrays):
    return lax.optimization_barrier(arrays)


def bf(*shape):
    return jax.ShapeDtypeStruct(shape, BF16)


def f32(*shape):
    return jax.ShapeDtypeStruct(shape, F32)


def call(kernel, outs, inputs, scalars=0, scratch=(), flops=0):
    vmem = pl.BlockSpec(memory_space=pltpu.VMEM)
    smem = pl.BlockSpec(memory_space=pltpu.SMEM)
    moved = sum(a.size * a.dtype.itemsize for a in inputs) + sum(
        o.size * o.dtype.itemsize for o in outs
    )
    held = sum(math.prod(s.shape) * 2 for s in scratch)
    got = pl.pallas_call(
        kernel,
        out_shape=outs,
        in_specs=[smem] * scalars + [vmem] * (len(inputs) - scalars),
        out_specs=(vmem,) * len(outs),
        scratch_shapes=scratch,
        cost_estimate=pl.CostEstimate(flops=flops, bytes_accessed=moved, transcendentals=0),
        compiler_params=pltpu.CompilerParams(vmem_limit_bytes=moved + held + (3 << 20)),
    )(*inputs)
    return got if len(outs) > 1 else got[0]


def local(
    tokens,
    out_grad,
    expert_ids,
    gate_values,
    master_gate_up,
    master_down,
    moment_gate_up,
    moment_down,
    second_gate_up,
    second_down,
):
    r = lax.axis_index("dp")
    z, y = r // 2, r % 2
    order = [(k, dy) for k in range(4) for dy in range(2)]
    columns = jnp.stack([((z + k) % 4) * 2 + (y ^ dy) for k, dy in order])
    half = ((lax.axis_index("expert") >> 1) & 1).reshape(1)

    gu = master_gate_up[0].astype(BF16)
    dn = pack_down(master_down[0].astype(BF16))
    own = jnp.concatenate([gu[:128], dn[:64], gu[128:], dn[64:]], axis=0)
    below, above, other = z_up(own), z_down(own), y_swap(own)
    near_aux, far_aux = call(
        route_kernel,
        (f32(8, TOK), f32(8, TOK)),
        (half, expert_ids.T, gate_values.astype(F32).T),
        scalars=1,
    )
    near = call(
        spread_kernel,
        (bf(HALF_SLOTS, 2 * WIDTH + EXTRA),),
        (columns, near_aux, tokens, out_grad),
        scalars=1,
    )
    below, above, other, far_aux, near, tok_next, grad_next = tie(
        below, above, other, far_aux, near, tokens, out_grad
    )

    up2, down2 = z_up(other), z_down(other)
    their_aux, their_tok = yh_swap(far_aux), yh_swap(tok_next)
    near = exchange(near)
    up2, down2, their_aux, their_tok, grad_next = tie(
        up2, down2, their_aux, their_tok, grad_next
    )

    up3, down3 = pass_on(below, above, up2, down2, 56 << 20)
    up3, down3, their_grad = z_up(up3), z_down(down3), yh_swap(grad_next)
    send_far = call(
        spread_tokens_kernel,
        (bf(HALF_SLOTS, WIDTH),),
        (columns, their_aux, their_tok),
        scalars=1,
    )
    send_far, near = tie(send_far, near)
    far_in = exchange(send_far)
    up3, down3, their_grad = tie(up3, down3, their_grad)
    send_far = call(spread_grads_kernel, (bf(HALF_SLOTS, WIDTH + EXTRA),), (their_aux, their_grad))
    send_far, far_in = tie(send_far, far_in)
    far_grad = exchange(send_far)
    weights = (own, other, below, above, up2, down2, up3, down3)

    act, slope, swish, down = call(
        forward_kernel,
        (
            bf(SLOTS, HIDDEN),
            bf(SLOTS, HIDDEN),
            bf(SLOTS, HIDDEN),
            bf(HIDDEN, WIDTH),
        ),
        (columns, near, far_in) + weights,
        scalars=1,
        flops=4_800_000_000,
    )
    proj, far_plane, scaled = call(
        backward_kernel,
        (bf(SLOTS, 2 * HIDDEN), bf(512, 1536), bf(SLOTS, WIDTH)),
        (near, far_in, far_grad, slope, swish, down),
        flops=3_600_000_000,
    )

    t_up = z_up(far_plane[256:384])
    t_down = z_down(far_plane[384:512])
    parts = call(
        parts_kernel,
        (bf(8, 128, 1536),),
        (columns, act, scaled),
        scalars=1,
        scratch=(pltpu.VMEM((HIDDEN, WIDTH), BF16),),
        flops=2_400_000_000,
    )
    t_y = y_swap(parts[5])
    above_plane, below_plane = call(
        planes_kernel,
        (bf(512, 1536),) * 2,
        (near, far_in, proj),
        flops=2_400_000_000,
    )
    t_up, t_down, t_y, above_plane, below_plane, late_proj = tie(
        t_up, t_down, t_y, above_plane, below_plane, proj
    )
    s_up, s_down = call(
        second_kernel,
        (bf(448, 1536), bf(448, 1536)),
        (far_plane, above_plane, below_plane, parts, t_up, t_down, t_y),
    )
    s_y = jnp.concatenate([parts[3], parts[7]], axis=0)
    t_up, t_down, t_y = z_up(s_up), z_down(s_down), y_swap(s_y)
    own_plane = call(
        own_plane_kernel, (bf(512, 1536),), (near, far_in, late_proj), flops=1_200_000_000
    )
    back = call(
        back_kernel,
        (bf(SLOTS, WIDTH + EXTRA),),
        (near, far_grad, act, late_proj, down) + weights,
        flops=7_200_000_000,
    )
    t_up, t_down, t_y, back, own_plane = tie(t_up, t_down, t_y, back, own_plane)
    s_up, s_down, s_y = call(
        third_kernel,
        (bf(384, 1536),) * 3,
        (above_plane, below_plane, own_plane, parts, t_up, t_down, t_y),
    )
    t_up, t_down, t_y = z_up(s_up), z_down(s_down), y_swap(s_y)
    returned = exchange(back)
    t_up, t_down, t_y = tie(t_up, t_down, t_y)
    state = (
        master_gate_up[0],
        master_down[0],
        moment_gate_up[0],
        moment_down[0],
        second_gate_up[0],
        second_down[0],
    )
    new_own = update_call(own_plane, parts, t_up, t_down, t_y, state)

    below, above, other = z_up(new_own), z_down(new_own), y_swap(new_own)
    grad_gate_up = add(own_plane[:256], t_up[:256], t_down[:256], t_y[:256])
    grad_down = unpack_down(add(parts[0], t_up[256:], t_down[256:], t_y[256:]))
    master_gu_next, moment_gu_next, second_gu_next = adam_update(
        state[0], state[2], state[4], grad_gate_up
    )
    master_dn_next, moment_dn_next, second_dn_next = adam_update(
        state[1], state[3], state[5], grad_down
    )
    near_sum, far_sum = call(
        collect_kernel,
        (f32(TOK, WIDTH + EXTRA), bf(TOK, WIDTH + EXTRA)),
        (near_aux, their_aux, returned),
        flops=1_700_000_000,
    )
    below, above, other, far_sum, *kept = tie(
        below,
        above,
        other,
        far_sum,
        master_gu_next,
        moment_gu_next,
        second_gu_next,
        master_dn_next,
        moment_dn_next,
        second_dn_next,
    )
    (
        master_gu_next,
        moment_gu_next,
        second_gu_next,
        master_dn_next,
        moment_dn_next,
        second_dn_next,
    ) = kept
    up2, down2 = z_up(other), z_down(other)
    far_sum = yh_swap(far_sum)

    pieces = [(i, (n, 0), (n, 192)) for n, i in enumerate((0, 1, 2, 6))]
    new_gate_up, new_down = place_shards(columns, (new_own, other, above, below), pieces)
    up2, down2, far_sum, new_gate_up, new_down = tie(up2, down2, far_sum, new_gate_up, new_down)
    up3, down3 = pass_on(below, above, up2, down2, 6 << 20)
    up3, down3 = z_up(up3), z_down(down3)
    new_gate_up, new_down = place_shards(
        columns,
        (down2, up2),
        [(3, (0, 0), (0, 192)), (7, (1, 0), (1, 192))],
        (new_gate_up, new_down),
    )
    input_grad, scores = call(
        finish_kernel,
        (bf(TOK, WIDTH), bf(TOK, EXTRA)),
        (columns, near_sum, far_sum),
        scalars=1,
    )
    up3, down3, new_gate_up, new_down, input_grad = tie(
        up3, down3, new_gate_up, new_down, input_grad
    )
    new_gate_up, new_down = place_shards(
        columns,
        (up3, down3),
        [(4, (0, 0), (1, 0)), (5, (0, 192), (1, 192))],
        (new_gate_up, new_down),
    )
    gate_grad = scores[:, :2]
    return (
        input_grad,
        gate_grad,
        new_gate_up[None],
        new_down[None],
        master_gu_next[None],
        master_dn_next[None],
        moment_gu_next[None],
        moment_dn_next[None],
        second_gu_next[None],
        second_dn_next[None],
    )


def solution(mesh):
    rows = P(("dp", "expert"), None)
    state = P("expert", "dp", None)
    whole = P("expert", None, None)
    return jax.shard_map(
        local,
        mesh=mesh,
        in_specs=(rows,) * 4 + (state,) * 6,
        out_specs=(rows, rows, whole, whole) + (state,) * 6,
        check_vma=False,
    )
```
